512 devices in a mesh: gx: 32 (over x, z), gy: 16 (over y, core).
Axes of the slice: x: 4, y: 8, z: 8, core: 2. Of those that a mesh axis runs over, the one named last changes fastest.
Arguments:
- tangent: float32 [512, 131072], P('gx', 'gy'), may hold values from -0.125 to 0.125
- well_of_obs: int32 [131072], P('gy'), may hold values from 0 to 31
- live_from: int32 [32], replicated, may hold values from 0 to 65535
- noise_std: float32 [32], replicated, may hold values from 0.3 to 3
- innovation: float32 [131072], P('gy'), may hold values from -6 to 6
- prior_factor: float32 [512, 512], P('gx'), as said below
- prior_info: float32 [512], replicated, may hold values from -6 to 6
Outputs:
- factors: float32 [16, 512, 512], P('gy', 'gx')
- estimates: float32 [16, 512], P('gy', 'gx')
The draws below stay inside these ranges and needn't reach their ends.
Inputs may be any that keep to these rules, and one draw needn't show every extreme that they name: `prior_factor`: upper triangular; its diagonal lies between 1 and 2.
All inputs are finite; a program needn't handle non-finite values.
Results may differ from the reference program's by a relative error of at most 0.0003.
Values sent between devices are 32-bit elements; how exact they have to be, the bound alone decides.
A program may use at most 128 MiB of HBM per device.

```python
import math
import jax
import jax.numpy as jnp
from jax import lax

P_SIZE = 512
WELLS = 32
WIN = 8192
M = 131072
N_GY = 16


def draw_prior_factor(key, part):
    key = jax.random.fold_in(key, 7)
    key_diag, key_off = jax.random.split(key)
    diagonal = jax.random.uniform(key_diag, (P_SIZE,), jnp.float32, 1.0, 2.0)
    offdiag = jax.random.truncated_normal(key_off, -3.0, 3.0, (P_SIZE, P_SIZE), jnp.float32) * (0.5 / math.sqrt(P_SIZE))
    return jnp.triu(offdiag, 1) + jnp.diag(diagonal)


def with_ends(array, rng, low, top_value):
    longest = array.shape.index(max(array.shape))
    spots = []
    for shift in (0, 1):
        where = [jax.random.randint(jax.random.fold_in(rng, axis), (), 0, length) for axis, length in enumerate(array.shape)]
        where[longest] = (where[longest] + shift) % array.shape[longest]
        spots.append(tuple(where))
    return array.at[spots[0]].set(low).at[spots[1]].set(top_value)


def spiked(drawn, rng, source, target, shards_of, factor):
    def block_of(axis_at):
        return (jnp.arange(drawn.shape[axis_at]) // (drawn.shape[axis_at] // shards_of)).reshape((-1,) + (1,) * (drawn.ndim - 1 - axis_at))

    near = jax.random.permutation(rng, shards_of)[block_of(target)]
    other_side = (block_of(target) + shards_of // 2) % shards_of
    return jnp.where((block_of(source) == near) | (block_of(source) == other_side), factor * drawn, drawn)


def level_of(stream_key, dims, shards, smallest, top_value):
    loudness = 1.0
    for axis_at, shards_of in shards:
        heights = jax.random.uniform(jax.random.fold_in(jax.random.fold_in(stream_key, 6), axis_at), (shards_of,), jnp.float32, smallest / len(shards), top_value / len(shards))
        loudness = loudness * jnp.repeat(jnp.exp(heights), dims[axis_at] // shards_of).reshape((-1,) + (1,) * (len(dims) - 1 - axis_at))
    return loudness


def gaussian(stream_key, extent, scale, bound, cuts=(), held_as=jnp.bfloat16):
    values = jax.random.normal(stream_key, extent, jnp.float32) * scale
    if len(cuts) > 0:
        values = level_of(stream_key, extent, cuts, -0.22, 0.18) * values
    return jnp.clip(values, min=-bound, max=bound).astype(held_as)


def gaussian_with(own_key, dims, width, reach, shards, heavy, kind=jnp.bfloat16):
    values = width * jax.random.normal(own_key, dims, jnp.float32)
    if shards:
        values = values * level_of(own_key, dims, shards, -0.22, 0.18)
    return jnp.clip(spiked(values, jax.random.fold_in(own_key, 3), *heavy), -reach, reach).astype(kind)


def setup_inputs(seed: int = 0) -> dict:
    streams_of = jax.random.split(jax.random.key(seed), 8)
    tangent = gaussian_with(streams_of[0], (P_SIZE, M), WIN ** -0.5, 0.125, ((0, 32), (1, 16)), (1, 0, 32, 2.75), jnp.float32)
    well_of_obs = with_ends(jax.random.randint(streams_of[1], (M,), 0, WELLS), jax.random.fold_in(streams_of[1], 1), 0, WELLS - 1).astype(jnp.int32)
    live_from = with_ends(jax.random.randint(streams_of[2], (WELLS,), 0, M // 2), jax.random.fold_in(streams_of[2], 1), 0, (M // 2) - 1).astype(jnp.int32)
    noise_std = jnp.clip(jnp.exp(jax.random.uniform(streams_of[3], (WELLS,), jnp.float32, math.log(0.3), math.log(3.0))), 0.3, 3.0)
    innovation = gaussian(streams_of[4], (M,), 1.0, 6.0, ((0, 16),), jnp.float32)
    prior_factor = draw_prior_factor(jax.random.fold_in(streams_of[7], 71), 0)
    prior_info = gaussian(streams_of[6], (P_SIZE,), 1.0, 6.0, (), jnp.float32)
    return {"tangent": tangent, "well_of_obs": well_of_obs, "live_from": live_from, "noise_std": noise_std, "innovation": innovation, "prior_factor": prior_factor, "prior_info": prior_info}


def reference(tangent, well_of_obs, live_from, noise_std, innovation, prior_factor, prior_info):
    row_index = jnp.arange(tangent.shape[1], dtype=jnp.int32)
    weight = jnp.where(row_index >= live_from[well_of_obs], 1.0 / noise_std[well_of_obs], 0.0)
    scaled_innovation = weight * innovation
    prior_gram = lax.dot_general(prior_factor.astype(jnp.float32), prior_factor.astype(jnp.float32), (((0,), (0,)), ((), ())), precision=lax.Precision.HIGHEST, preferred_element_type=jnp.float32)
    prior_vector = jnp.dot(prior_info.astype(jnp.float32), prior_factor.astype(jnp.float32), precision=lax.Precision.HIGHEST, preferred_element_type=jnp.float32)

    def one_window(running, window_index):
        matrix, vector = running
        start = (window_index * WIN).astype(jnp.int32)
        tangent_block = lax.dynamic_slice_in_dim(tangent, start, WIN, 1)
        weight_block = lax.dynamic_slice_in_dim(weight, start, WIN, 0)
        innov_block = lax.dynamic_slice_in_dim(scaled_innovation, start, WIN, 0)
        whitened = tangent_block * weight_block[None, :]
        matrix = matrix + lax.dot_general(whitened.astype(jnp.float32), whitened.astype(jnp.float32), (((1,), (1,)), ((), ())), precision=lax.Precision.HIGHEST, preferred_element_type=jnp.float32)
        vector = vector + jnp.dot(whitened.astype(jnp.float32), innov_block.astype(jnp.float32), precision=lax.Precision.HIGHEST, preferred_element_type=jnp.float32)
        lower_factor = jnp.linalg.cholesky(matrix)
        forward = lax.linalg.triangular_solve(lower_factor, vector[:, None], left_side=True, lower=True)
        estimate = lax.linalg.triangular_solve(lower_factor, forward, left_side=True, lower=True, transpose_a=True)[:, 0]
        return ((matrix, vector), (lower_factor.T, estimate))
    finished, outputs = lax.scan(one_window, (prior_gram, prior_vector), jnp.arange(N_GY, dtype=jnp.int32))
    return (outputs[0], outputs[1])
```

```python
import functools

import jax
import jax.numpy as jnp
from jax import lax
from jax.experimental import pallas as pl
from jax.experimental.pallas import tpu as pltpu
from jax.sharding import PartitionSpec as P

MESH = pl.DeviceIdType.MESH
HIGHEST = lax.Precision.HIGHEST
B = 128


def pairs(blocks):
    return [(i, j) for i in range(blocks) for j in range(i, blocks)]


def nt(a, b):
    return lax.dot_general(
        a, b, (((1,), (1,)), ((), ())), precision=HIGHEST, preferred_element_type=jnp.float32
    )


def gather_kernel(
    nx, ny,
    tangent, well, live_from, noise_std, innovation, prior, prior_info,
    full,
    got, part, shards, earlier, total,
    send_a, recv_a, send_b, recv_b, send_c, recv_c, send_d, recv_d, own_sem,
):
    gx, gy = lax.axis_index("gx"), lax.axis_index("gy")
    rows, obs = tangent.shape
    size = rows * nx
    share = obs // nx
    blocks = size // B
    halves = share // B
    cut = part.shape[0] // nx

    def at_x(step):
        return lax.rem(gx + step, nx)

    barrier = pltpu.get_barrier_semaphore()

    @pl.loop(1, nx)
    def _(step):
        pl.semaphore_signal(barrier, inc=1, device_id=(at_x(step), gy), device_id_type=MESH)

    @pl.loop(1, ny)
    def _(step):
        pl.semaphore_signal(
            barrier, inc=1, device_id=(gx, lax.rem(gy + step, ny)), device_id_type=MESH
        )

    pl.semaphore_wait(barrier, nx + ny - 2)

    def piece(peer):
        return tangent.at[:, pl.ds(pl.multiple_of(peer * share, share), share)]

    def slot(owner):
        return got.at[pl.ds(pl.multiple_of(owner * rows, rows), rows), :]

    def swap(step):
        peer = at_x(step)
        return pltpu.make_async_remote_copy(
            src_ref=piece(peer), dst_ref=slot(gx),
            send_sem=send_a.at[step], recv_sem=recv_a.at[step],
            device_id=(peer, gy), device_id_type=MESH,
        )

    @pl.loop(1, nx)
    def _(step):
        swap(step).start()

    own = pltpu.make_async_copy(piece(gx), slot(gx), own_sem)
    own.start()

    wells = well[pl.ds(halves * gx, halves), :]
    row_index = (
        gy * obs + gx * share
        + B * lax.broadcasted_iota(jnp.int32, (halves, B), 0)
        + lax.broadcasted_iota(jnp.int32, (halves, B), 1)
    )
    starts = jnp.zeros((halves, B), jnp.int32)
    noise = jnp.ones((halves, B), jnp.float32)
    for k in range(live_from.shape[0]):
        here = wells == k
        starts = jnp.where(here, live_from[k], starts)
        noise = jnp.where(here, noise_std[k], noise)
    weight = jnp.where(row_index >= starts, 1.0 / noise, 0.0)
    scaled = weight * innovation[pl.ds(halves * gx, halves), :]

    first = jnp.where(gy == 0, 1.0, 0.0).astype(jnp.float32)
    moment = jnp.zeros((1, size), jnp.float32)
    for k in range(rows):
        moment = moment + prior_info[gx * rows + k] * prior[k : k + 1, :]
    moment = first * moment
    prior_t = first * jnp.transpose(prior[...])

    own.wait()

    @pl.loop(1, nx)
    def _(step):
        swap(step).wait()

    whitened = [got[:, h * B : (h + 1) * B] * weight[h : h + 1, :] for h in range(halves)]
    for h in range(halves):
        moment = moment + nt(jnp.broadcast_to(scaled[h : h + 1, :], (8, B)), whitened[h])[0:1, :]
    lanes = lax.broadcasted_iota(jnp.int32, (B, B), 1)
    subs = lax.broadcasted_iota(jnp.int32, (B, B), 0)
    row = 0
    for i in range(blocks):
        lo = i * B
        strip = nt(prior_t[lo : lo + B], prior_t[lo:])
        for h in range(halves):
            strip = strip + nt(whitened[h][lo : lo + B], whitened[h][lo:])
        for j in range(i, blocks):
            tile = strip[:, (j - i) * B : (j - i + 1) * B]
            if i == j:
                vector = moment[:, lo : lo + B]
                last = vector[:, B - 1 : B]
                tile = jnp.where(subs > lanes, jnp.where(subs == B - 1, vector, last), tile)
            part[row : row + B, :] = tile
            row += B

    def shard(peer):
        return pl.ds(pl.multiple_of(peer * cut, 8), cut)

    def scatter(step):
        peer = at_x(step)
        return pltpu.make_async_remote_copy(
            src_ref=part.at[shard(peer), :], dst_ref=shards.at[step],
            send_sem=send_b.at[step], recv_sem=recv_b.at[step],
            device_id=(peer, gy), device_id_type=MESH,
        )

    @pl.loop(1, nx)
    def _(step):
        scatter(step).start()

    def take(step, acc):
        scatter(step).wait()
        return acc + shards[step]

    total[...] = lax.fori_loop(1, nx, take, part[shard(gx), :])

    def later(step):
        return pltpu.make_async_remote_copy(
            src_ref=total, dst_ref=earlier.at[step],
            send_sem=send_c.at[step], recv_sem=recv_c.at[step],
            device_id=(gx, lax.rem(gy + step, ny)), device_id_type=MESH,
        )

    @pl.loop(1, ny - gy)
    def _(step):
        later(step).start()

    def before(step, acc):
        later(step).wait_recv()
        return acc + earlier[step]

    full[shard(gx), :] = lax.fori_loop(1, gy + 1, before, total[...])

    def share_out(step):
        return pltpu.make_async_remote_copy(
            src_ref=full.at[shard(gx), :], dst_ref=full.at[shard(gx), :],
            send_sem=send_d.at[step], recv_sem=recv_d.at[step],
            device_id=(at_x(step), gy), device_id_type=MESH,
        )

    @pl.loop(1, nx)
    def _(step):
        share_out(step).start()

    @pl.loop(1, ny - gy)
    def _(step):
        later(step).wait_send()

    @pl.loop(1, nx)
    def _(step):
        share_out(step).wait()


def gathered(nx, ny, tangent, well, live_from, noise_std, innovation, prior, prior_info):
    rows, obs = tangent.shape
    size = rows * nx
    packed = len(pairs(size // B)) * B
    vmem = pl.BlockSpec(memory_space=pltpu.VMEM)
    smem = pl.BlockSpec(memory_space=pltpu.SMEM)
    hbm = pl.BlockSpec(memory_space=pl.ANY)
    dma = pltpu.SemaphoreType.DMA
    return pl.pallas_call(
        functools.partial(gather_kernel, nx, ny),
        out_shape=jax.ShapeDtypeStruct((packed, B), jnp.float32),
        in_specs=[hbm, vmem, smem, smem, vmem, vmem, smem],
        out_specs=vmem,
        scratch_shapes=[
            pltpu.VMEM((size, obs // nx), jnp.float32),
            pltpu.VMEM((packed, B), jnp.float32),
            pltpu.VMEM((nx, packed // nx, B), jnp.float32),
            pltpu.VMEM((ny, packed // nx, B), jnp.float32),
            pltpu.VMEM((packed // nx, B), jnp.float32),
            dma((nx,)), dma((nx,)), dma((nx,)), dma((nx,)),
            dma((ny,)), dma((ny,)), dma((nx,)), dma((nx,)),
            dma,
        ],
        compiler_params=pltpu.CompilerParams(
            collective_id=0, has_side_effects=True, vmem_limit_bytes=32 * 2**20
        ),
        name="gather",
    )(tangent, well, live_from, noise_std, innovation, prior, prior_info)


def body(nx, ny, tangent, well_of_obs, live_from, noise_std, innovation, prior_factor, prior_info):
    column = lax.axis_index("gx")
    rows = prior_factor.shape[0]
    size = rows * nx
    packed = gathered(
        nx, ny, tangent, well_of_obs.reshape(-1, B), live_from, noise_std,
        innovation.reshape(-1, B), prior_factor, prior_info,
    )
    blocks = size // B
    upper = {p: packed[k * B : (k + 1) * B] for k, p in enumerate(pairs(blocks))}
    vector = jnp.concatenate(
        [
            jnp.concatenate([upper[i, i][B - 1, : B - 1], upper[i, i][B - 2, :1]])
            for i in range(blocks)
        ]
    )
    for i in range(blocks):
        top = jnp.triu(upper[i, i])
        upper[i, i] = top + jnp.triu(top, 1).T
    matrix = jnp.concatenate(
        [
            jnp.concatenate([upper[i, j] if i <= j else upper[j, i].T for j in range(blocks)], 1)
            for i in range(blocks)
        ],
        0,
    )
    lower_factor = jnp.linalg.cholesky(matrix)
    forward = lax.linalg.triangular_solve(lower_factor, vector[:, None], left_side=True, lower=True)
    estimate = lax.linalg.triangular_solve(
        lower_factor, forward, left_side=True, lower=True, transpose_a=True
    )[:, 0]
    factor_rows = lax.dynamic_slice_in_dim(lower_factor, column * rows, rows, 1).T
    estimate_part = lax.dynamic_slice_in_dim(estimate, column * rows, rows, 0)
    return (factor_rows[None, :, :], estimate_part[None, :])


def solution(mesh):
    in_specs = (P("gx", "gy"), P("gy"), P(), P(), P("gy"), P("gx", None), P())
    out_specs = (P("gy", "gx", None), P("gy", "gx"))
    nx, ny = mesh.shape["gx"], mesh.shape["gy"]
    return jax.shard_map(
        functools.partial(body, nx, ny), mesh=mesh, in_specs=in_specs, out_specs=out_specs, check_vma=False
    )
```

```python
import functools

import jax
import jax.numpy as jnp
from jax import lax
from jax.experimental import pallas as pl
from jax.experimental.pallas import tpu as pltpu
from jax.sharding import PartitionSpec as P

MESH = pl.DeviceIdType.MESH
HIGHEST = lax.Precision.HIGHEST
B = 128


def pairs(blocks):
    return [(i, j) for i in range(blocks) for j in range(i, blocks)]


def nt(a, b):
    return lax.dot_general(
        a, b, (((1,), (1,)), ((), ())), precision=HIGHEST, preferred_element_type=jnp.float32
    )


def gather_kernel(
    nx, ny,
    tangent, well, live_from, noise_std, innovation, prior, prior_info,
    full,
    got, part, shards, earlier, total,
    send_a, recv_a, send_b, recv_b, send_c, recv_c, send_d, recv_d, own_sem,
):
    gx, gy = lax.axis_index("gx"), lax.axis_index("gy")
    rows, obs = tangent.shape
    size = rows * nx
    share = obs // nx
    blocks = size // B
    halves = share // B
    cut = part.shape[0] // nx

    def at_x(step):
        return lax.rem(gx + step, nx)

    barrier = pltpu.get_barrier_semaphore()

    @pl.loop(1, nx)
    def _(step):
        pl.semaphore_signal(barrier, inc=1, device_id=(at_x(step), gy), device_id_type=MESH)

    @pl.loop(1, ny)
    def _(step):
        pl.semaphore_signal(
            barrier, inc=1, device_id=(gx, lax.rem(gy + step, ny)), device_id_type=MESH
        )

    pl.semaphore_wait(barrier, nx + ny - 2)

    def piece(peer):
        return tangent.at[:, pl.ds(pl.multiple_of(peer * share, share), share)]

    def slot(owner):
        return got.at[pl.ds(pl.multiple_of(owner * rows, rows), rows), :]

    def swap(step):
        peer = at_x(step)
        return pltpu.make_async_remote_copy(
            src_ref=piece(peer), dst_ref=slot(gx),
            send_sem=send_a.at[step], recv_sem=recv_a.at[step],
            device_id=(peer, gy), device_id_type=MESH,
        )

    @pl.loop(1, nx)
    def _(step):
        swap(step).start()

    own = pltpu.make_async_copy(piece(gx), slot(gx), own_sem)
    own.start()

    wells = well[pl.ds(halves * gx, halves), :]
    row_index = (
        gy * obs + gx * share
        + B * lax.broadcasted_iota(jnp.int32, (halves, B), 0)
        + lax.broadcasted_iota(jnp.int32, (halves, B), 1)
    )
    starts = jnp.zeros((halves, B), jnp.int32)
    noise = jnp.ones((halves, B), jnp.float32)
    for k in range(live_from.shape[0]):
        here = wells == k
        starts = jnp.where(here, live_from[k], starts)
        noise = jnp.where(here, noise_std[k], noise)
    weight = jnp.where(row_index >= starts, 1.0 / noise, 0.0)
    scaled = weight * innovation[pl.ds(halves * gx, halves), :]

    first = jnp.where(gy == 0, 1.0, 0.0).astype(jnp.float32)
    moment = jnp.zeros((1, size), jnp.float32)
    for k in range(rows):
        moment = moment + prior_info[gx * rows + k] * prior[k : k + 1, :]
    moment = first * moment
    prior_t = first * jnp.transpose(prior[...])

    own.wait()

    @pl.loop(1, nx)
    def _(step):
        swap(step).wait()

    whitened = [got[:, h * B : (h + 1) * B] * weight[h : h + 1, :] for h in range(halves)]
    for h in range(halves):
        moment = moment + nt(jnp.broadcast_to(scaled[h : h + 1, :], (8, B)), whitened[h])[0:1, :]
    lanes = lax.broadcasted_iota(jnp.int32, (B, B), 1)
    subs = lax.broadcasted_iota(jnp.int32, (B, B), 0)
    row = 0
    for i in range(blocks):
        lo = i * B
        strip = nt(prior_t[lo : lo + B], prior_t[lo:])
        for h in range(halves):
            strip = strip + nt(whitened[h][lo : lo + B], whitened[h][lo:])
        for j in range(i, blocks):
            tile = strip[:, (j - i) * B : (j - i + 1) * B]
            if i == j:
                vector = moment[:, lo : lo + B]
                last = vector[:, B - 1 : B]
                tile = jnp.where(subs > lanes, jnp.where(subs == B - 1, vector, last), tile)
            part[row : row + B, :] = tile
            row += B

    def shard(peer):
        return pl.ds(pl.multiple_of(peer * cut, 8), cut)

    def scatter(step):
        peer = at_x(step)
        return pltpu.make_async_remote_copy(
            src_ref=part.at[shard(peer), :], dst_ref=shards.at[step],
            send_sem=send_b.at[step], recv_sem=recv_b.at[step],
            device_id=(peer, gy), device_id_type=MESH,
        )

    @pl.loop(1, nx)
    def _(step):
        scatter(step).start()

    def take(step, acc):
        scatter(step).wait()
        return acc + shards[step]

    total[...] = lax.fori_loop(1, nx, take, part[shard(gx), :])

    def later(step):
        return pltpu.make_async_remote_copy(
            src_ref=total, dst_ref=earlier.at[step],
            send_sem=send_c.at[step], recv_sem=recv_c.at[step],
            device_id=(gx, lax.rem(gy + step, ny)), device_id_type=MESH,
        )

    @pl.loop(1, ny - gy)
    def _(step):
        later(step).start()

    def before(step, acc):
        later(step).wait_recv()
        return acc + earlier[step]

    full[shard(gx), :] = lax.fori_loop(1, gy + 1, before, total[...])

    def share_out(step):
        return pltpu.make_async_remote_copy(
            src_ref=full.at[shard(gx), :], dst_ref=full.at[shard(gx), :],
            send_sem=send_d.at[step], recv_sem=recv_d.at[step],
            device_id=(at_x(step), gy), device_id_type=MESH,
        )

    @pl.loop(1, nx)
    def _(step):
        share_out(step).start()

    @pl.loop(1, ny - gy)
    def _(step):
        later(step).wait_send()

    @pl.loop(1, nx)
    def _(step):
        share_out(step).wait()


def gathered(nx, ny, tangent, well, live_from, noise_std, innovation, prior, prior_info):
    rows, obs = tangent.shape
    size = rows * nx
    packed = len(pairs(size // B)) * B
    vmem = pl.BlockSpec(memory_space=pltpu.VMEM)
    smem = pl.BlockSpec(memory_space=pltpu.SMEM)
    hbm = pl.BlockSpec(memory_space=pl.ANY)
    dma = pltpu.SemaphoreType.DMA
    return pl.pallas_call(
        functools.partial(gather_kernel, nx, ny),
        out_shape=jax.ShapeDtypeStruct((packed, B), jnp.float32),
        in_specs=[hbm, vmem, smem, smem, vmem, vmem, smem],
        out_specs=vmem,
        scratch_shapes=[
            pltpu.VMEM((size, obs // nx), jnp.float32),
            pltpu.VMEM((packed, B), jnp.float32),
            pltpu.VMEM((nx, packed // nx, B), jnp.float32),
            pltpu.VMEM((ny, packed // nx, B), jnp.float32),
            pltpu.VMEM((packed // nx, B), jnp.float32),
            dma((nx,)), dma((nx,)), dma((nx,)), dma((nx,)),
            dma((ny,)), dma((ny,)), dma((nx,)), dma((nx,)),
            dma,
        ],
        compiler_params=pltpu.CompilerParams(
            collective_id=0, has_side_effects=True, vmem_limit_bytes=32 * 2**20
        ),
        name="gather",
    )(tangent, well, live_from, noise_std, innovation, prior, prior_info)


def mm(a, b, dims):
    return lax.dot_general(
        a, b, (dims, ((), ())), precision=HIGHEST, preferred_element_type=jnp.float32
    )


NN = ((1,), (0,))
NT = ((1,), (1,))


def splat(row):
    return jnp.broadcast_to(row, (8, B))


def factor_block(s, width):
    tiles = width // 8
    sub = lax.broadcasted_iota(jnp.int32, (8, B), 0)
    lanes = lax.broadcasted_iota(jnp.int32, (B, B), 1)
    subs = lax.broadcasted_iota(jnp.int32, (B, B), 0)
    rest = jnp.concatenate([s, jnp.where(subs == lanes, 1.0, 0.0).astype(jnp.float32)], axis=1)
    done = []
    for lo in range(0, B, width):
        columns = [
            [
                jnp.broadcast_to(rest[8 * t : 8 * t + 8, lo + j : lo + j + 1], (8, B)) if t >= j // 8 else None
                for t in range(tiles)
            ]
            for j in range(width)
        ]
        panel = [[rest[8 * t : 8 * t + 8, h * B : (h + 1) * B] for h in range(2)] for t in range(tiles)]
        pivots = [jnp.ones((8, B), jnp.float32) for _ in range(tiles)]
        for k in range(width):
            tk, rk = divmod(k, 8)
            column = columns[k]
            pivot = splat(column[tk][rk : rk + 1])
            inverse = 1.0 / pivot
            pivots[tk] = jnp.where(sub == rk, pivot, pivots[tk])
            scaled = [column[t] * inverse if t >= tk else None for t in range(tiles)]
            for j in range(k + 1, width):
                tj, rj = divmod(j, 8)
                factor = splat(scaled[tj][rj : rj + 1])
                for t in range(tj, tiles):
                    columns[j][t] = columns[j][t] - column[t] * factor
            scaled[tk] = jnp.where(sub > rk, scaled[tk], 0.0)
            for h in range(2):
                row = splat(panel[tk][h][rk : rk + 1])
                for t in range(tk, tiles):
                    panel[t][h] = panel[t][h] - scaled[t] * row
        rows = jnp.concatenate(
            [
                jnp.concatenate([panel[t][h] * lax.rsqrt(pivots[t]) for h in range(2)], axis=1)
                for t in range(tiles)
            ],
            axis=0,
        )
        done.append(rows)
        if lo + width < B:
            left = jnp.transpose(rows[:, :B])[lo + width :]
            rest = rest[width:] - mm(left, rows, NN)
    both = jnp.concatenate(done, axis=0)
    return jnp.where(subs <= lanes, both[:, :B], 0.0), both[:, B:]


def factor_kernel(blocks, packed, rows_out, estimate_out, factor, answer):
    gx = lax.axis_index("gx")
    count = rows_out.shape[0]
    lanes = lax.broadcasted_iota(jnp.int32, (B, B), 1)
    subs = lax.broadcasted_iota(jnp.int32, (B, B), 0)
    lane = lax.broadcasted_iota(jnp.int32, (8, B), 1)
    s, vector = {}, []
    for k, (i, j) in enumerate(pairs(blocks)):
        tile = packed[k * B : (k + 1) * B, :]
        if i == j:
            vector.append(jnp.where(lane == B - 1, splat(tile[B - 2 : B - 1, 0:1]), splat(tile[B - 1 : B, :])))
            tile = jnp.where(subs <= lanes, tile, jnp.transpose(jnp.where(subs < lanes, tile, 0.0)))
        s[i, j] = tile
    factor[...] = jnp.zeros_like(factor)
    forward, inverse, right = [], [], {}
    for i in range(blocks):
        lo, hi = i * B, (i + 1) * B
        r, t = factor_block(s[i, i], 32)
        factor[lo:hi, lo:hi] = r
        inverse.append(t)
        forward.append(mm(vector[i], t, NT))
        if i + 1 < blocks:
            strip = mm(t, jnp.concatenate([s[i, j] for j in range(i + 1, blocks)], axis=1), NN)
            factor[lo:hi, hi:] = strip
            for j in range(i + 1, blocks):
                at = (j - i - 1) * B
                right[i, j] = strip[:, at : at + B]
                update = mm(jnp.transpose(right[i, j]), strip[:, at:], NN)
                for k in range(j, blocks):
                    s[j, k] = s[j, k] - update[:, (k - j) * B : (k - j + 1) * B]
            update = mm(forward[i], strip, NN)
            for j in range(i + 1, blocks):
                vector[j] = vector[j] - update[:, (j - i - 1) * B : (j - i) * B]
    x = [None] * blocks
    for i in reversed(range(blocks)):
        z = forward[i]
        for j in range(i + 1, blocks):
            z = z - mm(x[j], right[i, j], NT)
        x[i] = mm(z, inverse[i], NN)
        answer[8 * i : 8 * i + 8, :] = x[i]
    rows_out[...] = factor[pl.ds(pl.multiple_of(gx * count, count), count), :]
    per = B // count
    mine = answer[pl.ds(pl.multiple_of(8 * lax.div(gx, per), 8), 8), :]
    shift = lax.rem(B - count * lax.rem(gx, per), B)
    estimate_out[...] = pltpu.roll(mine, shift, 1)[0:1, :count]


def body(nx, ny, tangent, well_of_obs, live_from, noise_std, innovation, prior_factor, prior_info):
    rows = prior_factor.shape[0]
    size = rows * nx
    blocks = size // B
    packed = gathered(
        nx, ny, tangent, well_of_obs.reshape(-1, B), live_from, noise_std,
        innovation.reshape(-1, B), prior_factor, prior_info,
    )
    vmem = pl.BlockSpec(memory_space=pltpu.VMEM)
    factor_rows, estimate_part = pl.pallas_call(
        functools.partial(factor_kernel, blocks),
        out_shape=[
            jax.ShapeDtypeStruct((rows, size), jnp.float32),
            jax.ShapeDtypeStruct((1, rows), jnp.float32),
        ],
        in_specs=[vmem],
        out_specs=[vmem, vmem],
        scratch_shapes=[pltpu.VMEM((size, size), jnp.float32), pltpu.VMEM((8 * blocks, B), jnp.float32)],
        compiler_params=pltpu.CompilerParams(vmem_limit_bytes=32 * 2**20),
        name="factor",
    )(packed)
    return (factor_rows[None, :, :], estimate_part)


def solution(mesh):
    in_specs = (P("gx", "gy"), P("gy"), P(), P(), P("gy"), P("gx", None), P())
    out_specs = (P("gy", "gx", None), P("gy", "gx"))
    nx, ny = mesh.shape["gx"], mesh.shape["gy"]
    return jax.shard_map(
        functools.partial(body, nx, ny), mesh=mesh, in_specs=in_specs, out_specs=out_specs, check_vma=False
    )
```

```python
import functools

import jax
import jax.numpy as jnp
from jax import lax
from jax.experimental import pallas as pl
from jax.experimental.pallas import tpu as pltpu
from jax.sharding import PartitionSpec as P

MESH = pl.DeviceIdType.MESH
HIGHEST = lax.Precision.HIGHEST
B = 128


def pairs(blocks):
    return [(i, j) for i in range(blocks) for j in range(i, blocks)]


def nt(a, b):
    return lax.dot_general(
        a, b, (((1,), (1,)), ((), ())), precision=HIGHEST, preferred_element_type=jnp.float32
    )


NZ = 8


def gather_kernel(
    nx, ny,
    tangent, well, live_from, noise_std, innovation, prior, prior_info,
    full,
    got, part, from_x, sums, from_z, earlier, total,
    well_v, innovation_v, prior_v, live_s, noise_s, info_s,
    in_sem, send_a, recv_a, send_x, recv_x, send_z, recv_z, send_y, recv_y, send_s, recv_s, send_t, recv_t,
):
    gx, gy = lax.axis_index("gx"), lax.axis_index("gy")
    x, z = lax.div(gx, NZ), lax.rem(gx, NZ)
    nc = nx // NZ
    rows, obs = tangent.shape
    size = rows * nx
    share = obs // nx
    blocks = size // B
    halves = share // B
    cut = part.shape[0] // nx

    def ring(at, by, n):
        return lax.rem(at + by + n, n)

    def x_peer(by):
        return ring(x, by, nc) * NZ + z

    def z_peer(by):
        return x * NZ + ring(z, by, NZ)

    def far(by, n):
        return min(by, n - by)

    hops = sorted(
        [(i, j) for i in range(nc) for j in range(NZ) if i or j],
        key=lambda d: (-far(d[1], NZ), -far(d[0], nc), d),
    )
    turns = sorted(range(1, NZ), key=lambda d: (-far(d, NZ), d))

    group = 8 // halves
    tile = pl.ds(pl.multiple_of(8 * lax.div(gx, group), 8), 8)
    loads = [
        pltpu.make_async_copy(src, dst, in_sem.at[k])
        for k, (src, dst) in enumerate(
            [
                (well.at[tile, :], well_v), (innovation.at[tile, :], innovation_v), (prior, prior_v),
                (live_from, live_s), (noise_std, noise_s), (prior_info, info_s),
            ]
        )
    ]
    for load in loads:
        load.start()

    def piece(peer):
        return tangent.at[:, pl.ds(pl.multiple_of(peer * share, share), share)]

    def slot(owner):
        return got.at[pl.ds(pl.multiple_of(owner * rows, rows), rows), :]

    own = pltpu.make_async_copy(piece(gx), slot(gx), in_sem.at[6])
    own.start()

    barrier = pltpu.get_barrier_semaphore()
    for i, j in hops:
        pl.semaphore_signal(
            barrier, inc=1, device_id=(ring(x, i, nc) * NZ + ring(z, j, NZ), gy), device_id_type=MESH
        )
    for step in range(1, ny):
        pl.semaphore_signal(barrier, inc=1, device_id=(gx, ring(gy, step, ny)), device_id_type=MESH)
    pl.semaphore_wait(barrier, nx + ny - 2)

    swaps = []
    for k, (i, j) in enumerate(hops):
        peer = ring(x, i, nc) * NZ + ring(z, j, NZ)
        copy = pltpu.make_async_remote_copy(
            src_ref=piece(peer), dst_ref=slot(gx), send_sem=send_a.at[k], recv_sem=recv_a.at[k],
            device_id=(peer, gy), device_id_type=MESH,
        )
        copy.start()
        swaps.append(copy)

    for load in loads:
        load.wait()
    at = halves * lax.rem(gx, group)
    wells = well_v[pl.ds(at, halves), :]
    row_index = (
        gy * obs + gx * share
        + B * lax.broadcasted_iota(jnp.int32, (halves, B), 0)
        + lax.broadcasted_iota(jnp.int32, (halves, B), 1)
    )
    starts = jnp.zeros((halves, B), jnp.int32)
    noise = jnp.ones((halves, B), jnp.float32)
    for k in range(live_from.shape[0]):
        here = wells == k
        starts = jnp.where(here, live_s[k], starts)
        noise = jnp.where(here, noise_s[k], noise)
    weight = jnp.where(row_index >= starts, 1.0 / noise, 0.0)
    scaled = weight * innovation_v[pl.ds(at, halves), :]

    first = jnp.where(gy == 0, 1.0, 0.0).astype(jnp.float32)
    moment = jnp.zeros((1, size), jnp.float32)
    for k in range(rows):
        moment = moment + info_s[gx * rows + k] * prior_v[k : k + 1, :]
    moment = first * moment
    prior_t = first * jnp.transpose(prior_v[...])

    own.wait()
    for copy in swaps:
        copy.wait()

    whitened = [got[:, h * B : (h + 1) * B] * weight[h : h + 1, :] for h in range(halves)]
    for h in range(halves):
        moment = moment + nt(jnp.broadcast_to(scaled[h : h + 1, :], (8, B)), whitened[h])[0:1, :]
    lanes = lax.broadcasted_iota(jnp.int32, (B, B), 1)
    subs = lax.broadcasted_iota(jnp.int32, (B, B), 0)
    row = 0
    for i in range(blocks):
        lo = i * B
        strip = nt(prior_t[lo : lo + B], prior_t[lo:])
        for h in range(halves):
            strip = strip + nt(whitened[h][lo : lo + B], whitened[h][lo:])
        for j in range(i, blocks):
            block = strip[:, (j - i) * B : (j - i + 1) * B]
            if i == j:
                vector = moment[:, lo : lo + B]
                last = vector[:, B - 1 : B]
                block = jnp.where(subs > lanes, jnp.where(subs == B - 1, vector, last), block)
            part[row : row + B, :] = block
            row += B

    def shard(at_x, at_z):
        return pl.ds(pl.multiple_of((at_z * nc + at_x) * cut, 8), cut)

    order = turns + [0]
    across = []
    for k, turn in enumerate(order):
        across.append([])
        for i in range(1, nc):
            copy = pltpu.make_async_remote_copy(
                src_ref=part.at[shard(ring(x, i, nc), ring(z, turn, NZ)), :], dst_ref=from_x.at[k, i - 1],
                send_sem=send_x.at[k, i - 1], recv_sem=recv_x.at[k, i - 1],
                device_id=(x_peer(i), gy), device_id_type=MESH,
            )
            copy.start()
            across[k].append(copy)
    along = []
    for k, turn in enumerate(order):
        acc = part[shard(x, ring(z, turn, NZ)), :]
        for i in range(1, nc):
            across[k][i - 1].wait_recv()
            acc = acc + from_x[k, i - 1]
        if turn:
            sums[k] = acc
            copy = pltpu.make_async_remote_copy(
                src_ref=sums.at[k], dst_ref=from_z.at[k], send_sem=send_z.at[k], recv_sem=recv_z.at[k],
                device_id=(z_peer(turn), gy), device_id_type=MESH,
            )
            copy.start()
            along.append(copy)
    for k, copy in enumerate(along):
        copy.wait_recv()
        acc = acc + from_z[k]
    total[...] = acc

    def later(step):
        return pltpu.make_async_remote_copy(
            src_ref=total, dst_ref=earlier.at[step],
            send_sem=send_y.at[step], recv_sem=recv_y.at[step],
            device_id=(gx, ring(gy, step, ny)), device_id_type=MESH,
        )

    @pl.loop(1, ny - gy)
    def _(step):
        later(step).start()

    def before(step, acc):
        later(step).wait_recv()
        return acc + earlier[step]

    mine = full.at[shard(x, z), :]
    mine[...] = lax.fori_loop(1, gy + 1, before, acc)

    outward = []
    for k, turn in enumerate(turns):
        copy = pltpu.make_async_remote_copy(
            src_ref=mine, dst_ref=mine, send_sem=send_s.at[k], recv_sem=recv_s.at[k],
            device_id=(z_peer(turn), gy), device_id_type=MESH,
        )
        copy.start()
        outward.append(copy)
    near = sorted(range(NZ - 1), key=lambda k: (far(turns[k], NZ), k))
    onward = []
    for n, k in enumerate([None] + near):
        turn = 0
        if k is not None:
            outward[k].wait_recv()
            turn = turns[k]
        block = full.at[shard(x, ring(z, -turn, NZ)), :]
        for i in range(1, nc):
            copy = pltpu.make_async_remote_copy(
                src_ref=block, dst_ref=block, send_sem=send_t.at[n, i - 1], recv_sem=recv_t.at[n, i - 1],
                device_id=(x_peer(i), gy), device_id_type=MESH,
            )
            copy.start()
            onward.append(copy)

    for copy in onward:
        copy.wait_recv()
    for copies in across:
        for copy in copies:
            copy.wait_send()
    for copy in along + outward + onward:
        copy.wait_send()

    @pl.loop(1, ny - gy)
    def _(step):
        later(step).wait_send()


def gathered(nx, ny, tangent, well, live_from, noise_std, innovation, prior, prior_info):
    rows, obs = tangent.shape
    size = rows * nx
    packed = len(pairs(size // B)) * B
    cut = packed // nx
    nc = nx // NZ
    vmem = pltpu.VMEM
    hbm = pl.BlockSpec(memory_space=pltpu.HBM)
    dma = pltpu.SemaphoreType.DMA
    return pl.pallas_call(
        functools.partial(gather_kernel, nx, ny),
        out_shape=jax.ShapeDtypeStruct((packed, B), jnp.float32),
        in_specs=[hbm] * 7,
        out_specs=pl.BlockSpec(memory_space=pltpu.VMEM),
        scratch_shapes=[
            vmem((size, obs // nx), jnp.float32),
            vmem((packed, B), jnp.float32),
            vmem((NZ, nc - 1, cut, B), jnp.float32),
            vmem((NZ - 1, cut, B), jnp.float32),
            vmem((NZ - 1, cut, B), jnp.float32),
            vmem((ny, cut, B), jnp.float32),
            vmem((cut, B), jnp.float32),
            vmem((8, B), jnp.int32),
            vmem((8, B), jnp.float32),
            vmem((rows, size), jnp.float32),
            pltpu.SMEM(live_from.shape, jnp.int32),
            pltpu.SMEM(noise_std.shape, jnp.float32),
            pltpu.SMEM(prior_info.shape, jnp.float32),
            dma((7,)),
            dma((nx - 1,)), dma((nx - 1,)),
            dma((NZ, nc - 1)), dma((NZ, nc - 1)),
            dma((NZ - 1,)), dma((NZ - 1,)),
            dma((ny,)), dma((ny,)),
            dma((NZ - 1,)), dma((NZ - 1,)),
            dma((NZ, nc - 1)), dma((NZ, nc - 1)),
        ],
        compiler_params=pltpu.CompilerParams(
            collective_id=0, has_side_effects=True, vmem_limit_bytes=56 * 2**20
        ),
        name="gather",
    )(tangent, well, live_from, noise_std, innovation, prior, prior_info)


def mm(a, b, dims):
    return lax.dot_general(
        a, b, (dims, ((), ())), precision=HIGHEST, preferred_element_type=jnp.float32
    )


NN = ((1,), (0,))
NT = ((1,), (1,))


def splat(row):
    return jnp.broadcast_to(row, (8, B))


def factor_block(s, width):
    tiles = width // 8
    sub = lax.broadcasted_iota(jnp.int32, (8, B), 0)
    lanes = lax.broadcasted_iota(jnp.int32, (B, B), 1)
    subs = lax.broadcasted_iota(jnp.int32, (B, B), 0)
    rest = jnp.concatenate([s, jnp.where(subs == lanes, 1.0, 0.0).astype(jnp.float32)], axis=1)
    done = []
    for lo in range(0, B, width):
        columns = [
            [
                jnp.broadcast_to(rest[8 * t : 8 * t + 8, lo + j : lo + j + 1], (8, B)) if t >= j // 8 else None
                for t in range(tiles)
            ]
            for j in range(width)
        ]
        panel = [[rest[8 * t : 8 * t + 8, h * B : (h + 1) * B] for h in range(2)] for t in range(tiles)]
        pivots = [jnp.ones((8, B), jnp.float32) for _ in range(tiles)]
        for k in range(width):
            tk, rk = divmod(k, 8)
            column = columns[k]
            pivot = splat(column[tk][rk : rk + 1])
            inverse = 1.0 / pivot
            pivots[tk] = jnp.where(sub == rk, pivot, pivots[tk])
            scaled = [column[t] * inverse if t >= tk else None for t in range(tiles)]
            for j in range(k + 1, width):
                tj, rj = divmod(j, 8)
                factor = splat(scaled[tj][rj : rj + 1])
                for t in range(tj, tiles):
                    columns[j][t] = columns[j][t] - column[t] * factor
            scaled[tk] = jnp.where(sub > rk, scaled[tk], 0.0)
            for h in range(2):
                row = splat(panel[tk][h][rk : rk + 1])
                for t in range(tk, tiles):
                    panel[t][h] = panel[t][h] - scaled[t] * row
        rows = jnp.concatenate(
            [
                jnp.concatenate([panel[t][h] * lax.rsqrt(pivots[t]) for h in range(2)], axis=1)
                for t in range(tiles)
            ],
            axis=0,
        )
        done.append(rows)
        if lo + width < B:
            left = jnp.transpose(rows[:, :B])[lo + width :]
            rest = rest[width:] - mm(left, rows, NN)
    both = jnp.concatenate(done, axis=0)
    return jnp.where(subs <= lanes, both[:, :B], 0.0), both[:, B:]


def factor_kernel(blocks, packed, rows_out, estimate_out, factor, answer):
    gx = lax.axis_index("gx")
    count = rows_out.shape[0]
    lanes = lax.broadcasted_iota(jnp.int32, (B, B), 1)
    subs = lax.broadcasted_iota(jnp.int32, (B, B), 0)
    lane = lax.broadcasted_iota(jnp.int32, (8, B), 1)
    s, vector = {}, []
    for k, (i, j) in enumerate(pairs(blocks)):
        tile = packed[k * B : (k + 1) * B, :]
        if i == j:
            vector.append(jnp.where(lane == B - 1, splat(tile[B - 2 : B - 1, 0:1]), splat(tile[B - 1 : B, :])))
            tile = jnp.where(subs <= lanes, tile, jnp.transpose(jnp.where(subs < lanes, tile, 0.0)))
        s[i, j] = tile
    factor[...] = jnp.zeros_like(factor)
    forward, inverse, right = [], [], {}
    for i in range(blocks):
        lo, hi = i * B, (i + 1) * B
        r, t = factor_block(s[i, i], 32)
        factor[lo:hi, lo:hi] = r
        inverse.append(t)
        forward.append(mm(vector[i], t, NT))
        if i + 1 < blocks:
            strip = mm(t, jnp.concatenate([s[i, j] for j in range(i + 1, blocks)], axis=1), NN)
            factor[lo:hi, hi:] = strip
            for j in range(i + 1, blocks):
                at = (j - i - 1) * B
                right[i, j] = strip[:, at : at + B]
                update = mm(jnp.transpose(right[i, j]), strip[:, at:], NN)
                for k in range(j, blocks):
                    s[j, k] = s[j, k] - update[:, (k - j) * B : (k - j + 1) * B]
            update = mm(forward[i], strip, NN)
            for j in range(i + 1, blocks):
                vector[j] = vector[j] - update[:, (j - i - 1) * B : (j - i) * B]
    x = [None] * blocks
    for i in reversed(range(blocks)):
        z = forward[i]
        for j in range(i + 1, blocks):
            z = z - mm(x[j], right[i, j], NT)
        x[i] = mm(z, inverse[i], NN)
        answer[8 * i : 8 * i + 8, :] = x[i]
    rows_out[...] = factor[pl.ds(pl.multiple_of(gx * count, count), count), :]
    per = B // count
    mine = answer[pl.ds(pl.multiple_of(8 * lax.div(gx, per), 8), 8), :]
    shift = lax.rem(B - count * lax.rem(gx, per), B)
    estimate_out[...] = pltpu.roll(mine, shift, 1)[0:1, :count]


def body(nx, ny, tangent, well_of_obs, live_from, noise_std, innovation, prior_factor, prior_info):
    rows = prior_factor.shape[0]
    size = rows * nx
    blocks = size // B
    packed = gathered(
        nx, ny, tangent, well_of_obs.reshape(-1, B), live_from, noise_std,
        innovation.reshape(-1, B), prior_factor, prior_info,
    )
    vmem = pl.BlockSpec(memory_space=pltpu.VMEM)
    factor_rows, estimate_part = pl.pallas_call(
        functools.partial(factor_kernel, blocks),
        out_shape=[
            jax.ShapeDtypeStruct((rows, size), jnp.float32),
            jax.ShapeDtypeStruct((1, rows), jnp.float32),
        ],
        in_specs=[vmem],
        out_specs=[vmem, vmem],
        scratch_shapes=[pltpu.VMEM((size, size), jnp.float32), pltpu.VMEM((8 * blocks, B), jnp.float32)],
        compiler_params=pltpu.CompilerParams(vmem_limit_bytes=56 * 2**20),
        name="factor",
    )(packed)
    return (factor_rows[None, :, :], estimate_part)


def solution(mesh):
    in_specs = (P("gx", "gy"), P("gy"), P(), P(), P("gy"), P("gx", None), P())
    out_specs = (P("gy", "gx", None), P("gy", "gx"))
    nx, ny = mesh.shape["gx"], mesh.shape["gy"]
    return jax.shard_map(
        functools.partial(body, nx, ny), mesh=mesh, in_specs=in_specs, out_specs=out_specs, check_vma=False
    )
```

```python
import functools

import jax
import jax.numpy as jnp
from jax import lax
from jax.experimental import pallas as pl
from jax.experimental.pallas import tpu as pltpu
from jax.sharding import PartitionSpec as P

MESH = pl.DeviceIdType.MESH
HIGHEST = lax.Precision.HIGHEST
B = 128


def pairs(blocks):
    return [(i, j) for i in range(blocks) for j in range(i, blocks)]


def nt(a, b):
    return lax.dot_general(
        a, b, (((1,), (1,)), ((), ())), precision=HIGHEST, preferred_element_type=jnp.float32
    )


def pieces(v):
    a = v.astype(jnp.bfloat16)
    rest = v - a.astype(jnp.float32)
    b = rest.astype(jnp.bfloat16)
    return a, b, (rest - b.astype(jnp.float32)).astype(jnp.bfloat16)


def left_of(v):
    a, b, c = pieces(v)
    return jnp.concatenate([a, a, b, a, c, b], axis=1)


def right_of(v):
    a, b, c = pieces(v)
    return jnp.concatenate([a, b, a, c, a, b], axis=1)


def nt_pieces(a, b):
    return lax.dot_general(a, b, (((1,), (1,)), ((), ())), preferred_element_type=jnp.float32)


NZ = 8


def gather_kernel(
    nx, ny,
    tangent, well, live_from, noise_std, innovation, prior, prior_info,
    full,
    got, part, from_x, sums, from_z, earlier, total, passed, partner,
    well_v, innovation_v, prior_v, live_s, noise_s, info_s,
    in_sem, send_a, recv_a, send_x, recv_x, send_z, recv_z, send_y, recv_y, send_s, recv_s, send_t, recv_t,
):
    gx, gy = lax.axis_index("gx"), lax.axis_index("gy")
    x, z = lax.div(gx, NZ), lax.rem(gx, NZ)
    nc = nx // NZ
    rows, obs = tangent.shape
    size = rows * nx
    share = obs // nx
    blocks = size // B
    halves = share // B
    cut = part.shape[0] // nx

    def ring(at, by, n):
        return lax.rem(at + by + n, n)

    def x_peer(by):
        return ring(x, by, nc) * NZ + z

    def z_peer(by):
        return x * NZ + ring(z, by, NZ)

    def far(by, n):
        return min(by, n - by)

    hops = sorted(
        [(i, j) for i in range(nc) for j in range(NZ) if i or j],
        key=lambda d: (-far(d[1], NZ), -far(d[0], nc), d),
    )
    turns = sorted(range(1, NZ), key=lambda d: (-far(d, NZ), d))

    group = 8 // halves
    tile = pl.ds(pl.multiple_of(8 * lax.div(gx, group), 8), 8)
    loads = [
        pltpu.make_async_copy(src, dst, in_sem.at[k])
        for k, (src, dst) in enumerate(
            [
                (well.at[tile, :], well_v), (innovation.at[tile, :], innovation_v), (prior, prior_v),
                (live_from, live_s), (noise_std, noise_s), (prior_info, info_s),
            ]
        )
    ]
    for load in loads:
        load.start()

    def piece(peer):
        return tangent.at[:, pl.ds(pl.multiple_of(peer * share, share), share)]

    def slot(owner):
        return got.at[pl.ds(pl.multiple_of(owner * rows, rows), rows), :]

    own = pltpu.make_async_copy(piece(gx), slot(gx), in_sem.at[6])
    own.start()

    barrier = pltpu.get_barrier_semaphore()
    for i, j in hops:
        pl.semaphore_signal(
            barrier, inc=1, device_id=(ring(x, i, nc) * NZ + ring(z, j, NZ), gy), device_id_type=MESH
        )
    core = lax.rem(gy, 2)
    other = gy + 1 - 2 * core
    for step in range(2, ny, 2):
        pl.semaphore_signal(barrier, inc=1, device_id=(gx, ring(gy, step, ny)), device_id_type=MESH)
    pl.semaphore_signal(barrier, inc=1, device_id=(gx, other), device_id_type=MESH)
    pl.semaphore_wait(barrier, nx - 1 + ny // 2)

    swaps = []
    for k, (i, j) in enumerate(hops):
        peer = ring(x, i, nc) * NZ + ring(z, j, NZ)
        copy = pltpu.make_async_remote_copy(
            src_ref=piece(peer), dst_ref=slot(gx), send_sem=send_a.at[k], recv_sem=recv_a.at[k],
            device_id=(peer, gy), device_id_type=MESH,
        )
        copy.start()
        swaps.append(copy)

    for load in loads:
        load.wait()
    at = halves * lax.rem(gx, group)
    wells = well_v[pl.ds(at, halves), :]
    row_index = (
        gy * obs + gx * share
        + B * lax.broadcasted_iota(jnp.int32, (halves, B), 0)
        + lax.broadcasted_iota(jnp.int32, (halves, B), 1)
    )
    starts = jnp.zeros((halves, B), jnp.int32)
    noise = jnp.ones((halves, B), jnp.float32)
    for k in range(live_from.shape[0]):
        here = wells == k
        starts = jnp.where(here, live_s[k], starts)
        noise = jnp.where(here, noise_s[k], noise)
    weight = jnp.where(row_index >= starts, 1.0 / noise, 0.0)
    scaled = weight * innovation_v[pl.ds(at, halves), :]

    first = jnp.where(gy == 0, 1.0, 0.0).astype(jnp.float32)
    moment = jnp.zeros((1, size), jnp.float32)
    for k in range(rows):
        moment = moment + info_s[gx * rows + k] * prior_v[k : k + 1, :]
    moment = first * moment
    prior_t = first * jnp.transpose(prior_v[...])
    starts_at = {}
    row = 0
    for i in range(blocks):
        strip = nt(prior_t[i * B : (i + 1) * B], prior_t[i * B :])
        for j in range(i, blocks):
            part[row : row + B, :] = strip[:, (j - i) * B : (j - i + 1) * B]
            starts_at[i, j] = row
            row += B
    scaled = left_of(jnp.concatenate([jnp.broadcast_to(scaled[h : h + 1, :], (16, B)) for h in range(halves)], axis=1))

    own.wait()
    for copy in swaps:
        copy.wait()

    whitened = jnp.concatenate([got[:, h * B : (h + 1) * B] * weight[h : h + 1, :] for h in range(halves)], axis=1)
    left, right = left_of(whitened), right_of(whitened)
    moment = moment + nt_pieces(scaled, right)[0:1, :]
    lanes = lax.broadcasted_iota(jnp.int32, (B, B), 1)
    subs = lax.broadcasted_iota(jnp.int32, (B, B), 0)
    for i in range(blocks):
        lo = i * B
        strip = nt_pieces(left[lo : lo + B], right[lo:])
        for j in range(i, blocks):
            row = starts_at[i, j]
            block = part[row : row + B, :] + strip[:, (j - i) * B : (j - i + 1) * B]
            if i == j:
                vector = moment[:, lo : lo + B]
                last = vector[:, B - 1 : B]
                block = jnp.where(subs > lanes, jnp.where(subs == B - 1, vector, last), block)
            part[row : row + B, :] = block

    def shard(at_x, at_z):
        return pl.ds(pl.multiple_of((at_z * nc + at_x) * cut, 8), cut)

    order = turns + [0]
    across = []
    for k, turn in enumerate(order):
        across.append([])
        for i in range(1, nc):
            copy = pltpu.make_async_remote_copy(
                src_ref=part.at[shard(ring(x, i, nc), ring(z, turn, NZ)), :], dst_ref=from_x.at[k, i - 1],
                send_sem=send_x.at[k, i - 1], recv_sem=recv_x.at[k, i - 1],
                device_id=(x_peer(i), gy), device_id_type=MESH,
            )
            copy.start()
            across[k].append(copy)
    along = []
    for k, turn in enumerate(order):
        acc = part[shard(x, ring(z, turn, NZ)), :]
        for i in range(1, nc):
            across[k][i - 1].wait_recv()
            acc = acc + from_x[k, i - 1]
        if turn:
            sums[k] = acc
            copy = pltpu.make_async_remote_copy(
                src_ref=sums.at[k], dst_ref=from_z.at[k], send_sem=send_z.at[k], recv_sem=recv_z.at[k],
                device_id=(z_peer(turn), gy), device_id_type=MESH,
            )
            copy.start()
            along.append(copy)
    for k, copy in enumerate(along):
        copy.wait_recv()
        acc = acc + from_z[k]
    total[...] = acc

    y = lax.div(gy, 2)

    def later(step):
        return pltpu.make_async_remote_copy(
            src_ref=total, dst_ref=earlier.at[step],
            send_sem=send_y.at[step], recv_sem=recv_y.at[step],
            device_id=(gx, ring(gy, 2 * step, ny)), device_id_type=MESH,
        )

    @pl.loop(1, ny // 2 - y)
    def _(step):
        later(step).start()

    def before(step, sum_):
        later(step).wait_recv()
        return sum_ + earlier[step]

    past = lax.fori_loop(1, y + 1, before, jnp.zeros_like(acc))
    passed[...] = jnp.where(core == 0, past + acc, past)
    exchange = pltpu.make_async_remote_copy(
        src_ref=passed, dst_ref=partner, send_sem=send_y.at[0], recv_sem=recv_y.at[0],
        device_id=(gx, other), device_id_type=MESH,
    )
    exchange.start()
    past = past + acc
    exchange.wait_recv()
    mine = full.at[shard(x, z), :]
    mine[...] = past + partner[...]

    outward = []
    for k, turn in enumerate(turns):
        copy = pltpu.make_async_remote_copy(
            src_ref=mine, dst_ref=mine, send_sem=send_s.at[k], recv_sem=recv_s.at[k],
            device_id=(z_peer(turn), gy), device_id_type=MESH,
        )
        copy.start()
        outward.append(copy)
    near = sorted(range(NZ - 1), key=lambda k: (far(turns[k], NZ), k))
    onward = []
    for n, k in enumerate([None] + near):
        turn = 0
        if k is not None:
            outward[k].wait_recv()
            turn = turns[k]
        block = full.at[shard(x, ring(z, -turn, NZ)), :]
        for i in range(1, nc):
            copy = pltpu.make_async_remote_copy(
                src_ref=block, dst_ref=block, send_sem=send_t.at[n, i - 1], recv_sem=recv_t.at[n, i - 1],
                device_id=(x_peer(i), gy), device_id_type=MESH,
            )
            copy.start()
            onward.append(copy)

    for copy in onward:
        copy.wait_recv()
    for copies in across:
        for copy in copies:
            copy.wait_send()
    for copy in along + [exchange] + outward + onward:
        copy.wait_send()

    @pl.loop(1, ny // 2 - y)
    def _(step):
        later(step).wait_send()


def gathered(nx, ny, tangent, well, live_from, noise_std, innovation, prior, prior_info):
    rows, obs = tangent.shape
    size = rows * nx
    packed = len(pairs(size // B)) * B
    cut = packed // nx
    nc = nx // NZ
    vmem = pltpu.VMEM
    hbm = pl.BlockSpec(memory_space=pltpu.HBM)
    dma = pltpu.SemaphoreType.DMA
    return pl.pallas_call(
        functools.partial(gather_kernel, nx, ny),
        out_shape=jax.ShapeDtypeStruct((packed, B), jnp.float32),
        in_specs=[hbm] * 7,
        out_specs=pl.BlockSpec(memory_space=pltpu.VMEM),
        scratch_shapes=[
            vmem((size, obs // nx), jnp.float32),
            vmem((packed, B), jnp.float32),
            vmem((NZ, nc - 1, cut, B), jnp.float32),
            vmem((NZ - 1, cut, B), jnp.float32),
            vmem((NZ - 1, cut, B), jnp.float32),
            vmem((ny // 2, cut, B), jnp.float32),
            vmem((cut, B), jnp.float32),
            vmem((cut, B), jnp.float32),
            vmem((cut, B), jnp.float32),
            vmem((8, B), jnp.int32),
            vmem((8, B), jnp.float32),
            vmem((rows, size), jnp.float32),
            pltpu.SMEM(live_from.shape, jnp.int32),
            pltpu.SMEM(noise_std.shape, jnp.float32),
            pltpu.SMEM(prior_info.shape, jnp.float32),
            dma((7,)),
            dma((nx - 1,)), dma((nx - 1,)),
            dma((NZ, nc - 1)), dma((NZ, nc - 1)),
            dma((NZ - 1,)), dma((NZ - 1,)),
            dma((ny // 2,)), dma((ny // 2,)),
            dma((NZ - 1,)), dma((NZ - 1,)),
            dma((NZ, nc - 1)), dma((NZ, nc - 1)),
        ],
        compiler_params=pltpu.CompilerParams(
            collective_id=0, has_side_effects=True, vmem_limit_bytes=56 * 2**20
        ),
        name="gather",
    )(tangent, well, live_from, noise_std, innovation, prior, prior_info)


def mm(a, b, dims):
    return lax.dot_general(
        a, b, (dims, ((), ())), precision=HIGHEST, preferred_element_type=jnp.float32
    )


NN = ((1,), (0,))
NT = ((1,), (1,))


def splat(row):
    return jnp.broadcast_to(row, (8, B))


def factor_block(s, width):
    tiles = width // 8
    sub = lax.broadcasted_iota(jnp.int32, (8, B), 0)
    lanes = lax.broadcasted_iota(jnp.int32, (B, B), 1)
    subs = lax.broadcasted_iota(jnp.int32, (B, B), 0)
    rest = jnp.concatenate([s, jnp.where(subs == lanes, 1.0, 0.0).astype(jnp.float32)], axis=1)
    done = []
    for lo in range(0, B, width):
        panel = [[rest[8 * t : 8 * t + 8, h * B : (h + 1) * B] for h in range(2)] for t in range(tiles)]
        pivots = [jnp.ones((8, B), jnp.float32) for _ in range(tiles)]

        def spread(g):
            at = lo + 8 * g
            return [
                [jnp.broadcast_to(panel[t][0][:, at + j : at + j + 1], (8, B)) if t >= g else None for t in range(tiles)]
                for j in range(8)
            ]

        columns = spread(0)
        for g in range(tiles):
            if g + 1 < tiles:
                columns = columns + spread(g + 1)
            for k in range(8 * g, 8 * g + 8, 2):
                r = k - 8 * g
                one, two = columns[k], columns[k + 1]
                a, b, c = splat(one[g][r : r + 1]), splat(one[g][r + 1 : r + 2]), splat(two[g][r + 1 : r + 2])
                det = a * c - b * b
                inverse, first = 1.0 / det, 1.0 / a
                pivots[g] = jnp.where(sub == r, a, jnp.where(sub == r + 1, det * first, pivots[g]))
                u = [(c * one[t] - b * two[t]) * inverse if t >= g else None for t in range(tiles)]
                v = [(a * two[t] - b * one[t]) * inverse if t >= g else None for t in range(tiles)]
                for j in range(k + 2, len(columns)):
                    tj, rj = divmod(j, 8)
                    p, q = splat(u[tj][rj : rj + 1]), splat(v[tj][rj : rj + 1])
                    for t in range(tj, tiles):
                        columns[j][t] = columns[j][t] - (one[t] * p + two[t] * q)
                u[g] = jnp.where(sub > r + 1, u[g], jnp.where(sub == r + 1, b * first, 0.0))
                v[g] = jnp.where(sub > r + 1, v[g], 0.0)
                for h in range(2):
                    p, q = splat(panel[g][h][r : r + 1]), splat(panel[g][h][r + 1 : r + 2])
                    for t in range(g, tiles):
                        panel[t][h] = panel[t][h] - (u[t] * p + v[t] * q)
        rows = jnp.concatenate(
            [
                jnp.concatenate([panel[t][h] * lax.rsqrt(pivots[t]) for h in range(2)], axis=1)
                for t in range(tiles)
            ],
            axis=0,
        )
        done.append(rows)
        if lo + width < B:
            left = jnp.transpose(rows[:, :B])[lo + width :]
            rest = rest[width:] - mm(left, rows, NN)
    both = jnp.concatenate(done, axis=0)
    return jnp.where(subs <= lanes, both[:, :B], 0.0), both[:, B:]


def factor_kernel(blocks, packed, rows_out, estimate_out, factor, answer):
    gx = lax.axis_index("gx")
    count = rows_out.shape[0]
    lanes = lax.broadcasted_iota(jnp.int32, (B, B), 1)
    subs = lax.broadcasted_iota(jnp.int32, (B, B), 0)
    lane = lax.broadcasted_iota(jnp.int32, (8, B), 1)
    s, vector = {}, []
    for k, (i, j) in enumerate(pairs(blocks)):
        tile = packed[k * B : (k + 1) * B, :]
        if i == j:
            vector.append(jnp.where(lane == B - 1, splat(tile[B - 2 : B - 1, 0:1]), splat(tile[B - 1 : B, :])))
            tile = jnp.where(subs <= lanes, tile, jnp.transpose(jnp.where(subs < lanes, tile, 0.0)))
        s[i, j] = tile
    factor[...] = jnp.zeros_like(factor)
    forward, inverse, right = [], [], {}
    for i in range(blocks):
        lo, hi = i * B, (i + 1) * B
        r, t = factor_block(s[i, i], 32)
        factor[lo:hi, lo:hi] = r
        inverse.append(t)
        forward.append(mm(vector[i], t, NT))
        if i + 1 < blocks:
            strip = mm(t, jnp.concatenate([s[i, j] for j in range(i + 1, blocks)], axis=1), NN)
            factor[lo:hi, hi:] = strip
            for j in range(i + 1, blocks):
                at = (j - i - 1) * B
                right[i, j] = strip[:, at : at + B]
                update = mm(jnp.transpose(right[i, j]), strip[:, at:], NN)
                for k in range(j, blocks):
                    s[j, k] = s[j, k] - update[:, (k - j) * B : (k - j + 1) * B]
            update = mm(forward[i], strip, NN)
            for j in range(i + 1, blocks):
                vector[j] = vector[j] - update[:, (j - i - 1) * B : (j - i) * B]
    x = [None] * blocks
    for i in reversed(range(blocks)):
        z = forward[i]
        for j in range(i + 1, blocks):
            z = z - mm(x[j], right[i, j], NT)
        x[i] = mm(z, inverse[i], NN)
        answer[8 * i : 8 * i + 8, :] = x[i]
    rows_out[...] = factor[pl.ds(pl.multiple_of(gx * count, count), count), :]
    per = B // count
    mine = answer[pl.ds(pl.multiple_of(8 * lax.div(gx, per), 8), 8), :]
    shift = lax.rem(B - count * lax.rem(gx, per), B)
    estimate_out[...] = pltpu.roll(mine, shift, 1)[0:1, :count]


def body(nx, ny, tangent, well_of_obs, live_from, noise_std, innovation, prior_factor, prior_info):
    rows = prior_factor.shape[0]
    size = rows * nx
    blocks = size // B
    packed = gathered(
        nx, ny, tangent, well_of_obs.reshape(-1, B), live_from, noise_std,
        innovation.reshape(-1, B), prior_factor, prior_info,
    )
    vmem = pl.BlockSpec(memory_space=pltpu.VMEM)
    factor_rows, estimate_part = pl.pallas_call(
        functools.partial(factor_kernel, blocks),
        out_shape=[
            jax.ShapeDtypeStruct((rows, size), jnp.float32),
            jax.ShapeDtypeStruct((1, rows), jnp.float32),
        ],
        in_specs=[vmem],
        out_specs=[vmem, vmem],
        scratch_shapes=[pltpu.VMEM((size, size), jnp.float32), pltpu.VMEM((8 * blocks, B), jnp.float32)],
        compiler_params=pltpu.CompilerParams(vmem_limit_bytes=56 * 2**20),
        name="factor",
    )(packed)
    return (factor_rows[None, :, :], estimate_part)


def solution(mesh):
    in_specs = (P("gx", "gy"), P("gy"), P(), P(), P("gy"), P("gx", None), P())
    out_specs = (P("gy", "gx", None), P("gy", "gx"))
    nx, ny = mesh.shape["gx"], mesh.shape["gy"]
    return jax.shard_map(
        functools.partial(body, nx, ny), mesh=mesh, in_specs=in_specs, out_specs=out_specs, check_vma=False
    )
```

```python
import functools

import jax
import jax.numpy as jnp
from jax import lax
from jax.experimental import pallas as pl
from jax.experimental.pallas import tpu as pltpu
from jax.sharding import PartitionSpec as P

MESH = pl.DeviceIdType.MESH
HIGHEST = lax.Precision.HIGHEST
B = 128


def pairs(blocks):
    return [(i, j) for i in range(blocks) for j in range(i, blocks)]


def nt(a, b):
    return lax.dot_general(
        a, b, (((1,), (1,)), ((), ())), precision=HIGHEST, preferred_element_type=jnp.float32
    )


def pieces(v):
    a = v.astype(jnp.bfloat16)
    rest = v - a.astype(jnp.float32)
    b = rest.astype(jnp.bfloat16)
    return a, b, (rest - b.astype(jnp.float32)).astype(jnp.bfloat16)


def left_of(v):
    a, b, c = pieces(v)
    return jnp.concatenate([a, a, b, a, c, b], axis=1)


def right_of(v):
    a, b, c = pieces(v)
    return jnp.concatenate([a, b, a, c, a, b], axis=1)


def nt_pieces(a, b):
    return lax.dot_general(a, b, (((1,), (1,)), ((), ())), preferred_element_type=jnp.float32)


NZ = 8


def gather_kernel(
    nx, ny,
    tangent, well, live_from, noise_std, innovation, prior, prior_info,
    rows_out, estimate_out,
    full, factor, answer,
    got, part, from_x, sums, from_z, earlier, total, passed, partner,
    well_v, innovation_v, prior_v, live_s, noise_s, info_s,
    in_sem, send_a, recv_a, send_x, recv_x, send_z, recv_z, send_y, recv_y, send_s, recv_s, send_t, recv_t,
):
    gx, gy = lax.axis_index("gx"), lax.axis_index("gy")
    x, z = lax.div(gx, NZ), lax.rem(gx, NZ)
    nc = nx // NZ
    rows, obs = tangent.shape
    size = rows * nx
    share = obs // nx
    blocks = size // B
    halves = share // B
    cut = part.shape[0] // nx

    def ring(at, by, n):
        return lax.rem(at + by + n, n)

    def x_peer(by):
        return ring(x, by, nc) * NZ + z

    def z_peer(by):
        return x * NZ + ring(z, by, NZ)

    def far(by, n):
        return min(by, n - by)

    hops = sorted(
        [(i, j) for i in range(nc) for j in range(NZ) if i or j],
        key=lambda d: (-far(d[1], NZ), -far(d[0], nc), d),
    )
    turns = sorted(range(1, NZ), key=lambda d: (-far(d, NZ), d))

    group = 8 // halves
    tile = pl.ds(pl.multiple_of(8 * lax.div(gx, group), 8), 8)
    loads = [
        pltpu.make_async_copy(src, dst, in_sem.at[k])
        for k, (src, dst) in enumerate(
            [
                (well.at[tile, :], well_v), (innovation.at[tile, :], innovation_v), (prior, prior_v),
                (live_from, live_s), (noise_std, noise_s), (prior_info, info_s),
            ]
        )
    ]
    for load in loads:
        load.start()

    def piece(peer):
        return tangent.at[:, pl.ds(pl.multiple_of(peer * share, share), share)]

    def slot(owner):
        return got.at[pl.ds(pl.multiple_of(owner * rows, rows), rows), :]

    own = pltpu.make_async_copy(piece(gx), slot(gx), in_sem.at[6])
    own.start()

    barrier = pltpu.get_barrier_semaphore()
    for i, j in hops:
        pl.semaphore_signal(
            barrier, inc=1, device_id=(ring(x, i, nc) * NZ + ring(z, j, NZ), gy), device_id_type=MESH
        )
    core = lax.rem(gy, 2)
    other = gy + 1 - 2 * core
    for step in range(2, ny, 2):
        pl.semaphore_signal(barrier, inc=1, device_id=(gx, ring(gy, step, ny)), device_id_type=MESH)
    pl.semaphore_signal(barrier, inc=1, device_id=(gx, other), device_id_type=MESH)
    pl.semaphore_wait(barrier, nx - 1 + ny // 2)

    swaps = []
    for k, (i, j) in enumerate(hops):
        peer = ring(x, i, nc) * NZ + ring(z, j, NZ)
        copy = pltpu.make_async_remote_copy(
            src_ref=piece(peer), dst_ref=slot(gx), send_sem=send_a.at[k], recv_sem=recv_a.at[k],
            device_id=(peer, gy), device_id_type=MESH,
        )
        copy.start()
        swaps.append(copy)

    for load in loads:
        load.wait()
    at = halves * lax.rem(gx, group)
    wells = well_v[pl.ds(at, halves), :]
    row_index = (
        gy * obs + gx * share
        + B * lax.broadcasted_iota(jnp.int32, (halves, B), 0)
        + lax.broadcasted_iota(jnp.int32, (halves, B), 1)
    )
    starts = jnp.zeros((halves, B), jnp.int32)
    noise = jnp.ones((halves, B), jnp.float32)
    for k in range(live_from.shape[0]):
        here = wells == k
        starts = jnp.where(here, live_s[k], starts)
        noise = jnp.where(here, noise_s[k], noise)
    weight = jnp.where(row_index >= starts, 1.0 / noise, 0.0)
    scaled = weight * innovation_v[pl.ds(at, halves), :]

    first = jnp.where(gy == 0, 1.0, 0.0).astype(jnp.float32)
    moment = jnp.zeros((1, size), jnp.float32)
    for k in range(rows):
        moment = moment + info_s[gx * rows + k] * prior_v[k : k + 1, :]
    moment = first * moment
    prior_t = first * jnp.transpose(prior_v[...])
    starts_at = {}
    row = 0
    for i in range(blocks):
        strip = nt(prior_t[i * B : (i + 1) * B], prior_t[i * B :])
        for j in range(i, blocks):
            part[row : row + B, :] = strip[:, (j - i) * B : (j - i + 1) * B]
            starts_at[i, j] = row
            row += B
    scaled = left_of(jnp.concatenate([jnp.broadcast_to(scaled[h : h + 1, :], (16, B)) for h in range(halves)], axis=1))

    own.wait()
    for copy in swaps:
        copy.wait()

    whitened = jnp.concatenate([got[:, h * B : (h + 1) * B] * weight[h : h + 1, :] for h in range(halves)], axis=1)
    left, right = left_of(whitened), right_of(whitened)
    moment = moment + nt_pieces(scaled, right)[0:1, :]
    lanes = lax.broadcasted_iota(jnp.int32, (B, B), 1)
    subs = lax.broadcasted_iota(jnp.int32, (B, B), 0)
    for i in range(blocks):
        lo = i * B
        strip = nt_pieces(left[lo : lo + B], right[lo:])
        for j in range(i, blocks):
            row = starts_at[i, j]
            block = part[row : row + B, :] + strip[:, (j - i) * B : (j - i + 1) * B]
            if i == j:
                vector = moment[:, lo : lo + B]
                last = vector[:, B - 1 : B]
                block = jnp.where(subs > lanes, jnp.where(subs == B - 1, vector, last), block)
            part[row : row + B, :] = block

    def shard(at_x, at_z):
        return pl.ds(pl.multiple_of((at_z * nc + at_x) * cut, 8), cut)

    order = turns + [0]
    across = []
    for k, turn in enumerate(order):
        across.append([])
        for i in range(1, nc):
            copy = pltpu.make_async_remote_copy(
                src_ref=part.at[shard(ring(x, i, nc), ring(z, turn, NZ)), :], dst_ref=from_x.at[k, i - 1],
                send_sem=send_x.at[k, i - 1], recv_sem=recv_x.at[k, i - 1],
                device_id=(x_peer(i), gy), device_id_type=MESH,
            )
            copy.start()
            across[k].append(copy)
    along = []
    for k, turn in enumerate(order):
        acc = part[shard(x, ring(z, turn, NZ)), :]
        for i in range(1, nc):
            across[k][i - 1].wait_recv()
            acc = acc + from_x[k, i - 1]
        if turn:
            sums[k] = acc
            copy = pltpu.make_async_remote_copy(
                src_ref=sums.at[k], dst_ref=from_z.at[k], send_sem=send_z.at[k], recv_sem=recv_z.at[k],
                device_id=(z_peer(turn), gy), device_id_type=MESH,
            )
            copy.start()
            along.append(copy)
    for k, copy in enumerate(along):
        copy.wait_recv()
        acc = acc + from_z[k]
    total[...] = acc

    y = lax.div(gy, 2)

    def later(step):
        return pltpu.make_async_remote_copy(
            src_ref=total, dst_ref=earlier.at[step],
            send_sem=send_y.at[step], recv_sem=recv_y.at[step],
            device_id=(gx, ring(gy, 2 * step, ny)), device_id_type=MESH,
        )

    @pl.loop(1, ny // 2 - y)
    def _(step):
        later(step).start()

    def before(step, sum_):
        later(step).wait_recv()
        return sum_ + earlier[step]

    past = lax.fori_loop(1, y + 1, before, jnp.zeros_like(acc))
    passed[...] = jnp.where(core == 0, past + acc, past)
    exchange = pltpu.make_async_remote_copy(
        src_ref=passed, dst_ref=partner, send_sem=send_y.at[0], recv_sem=recv_y.at[0],
        device_id=(gx, other), device_id_type=MESH,
    )
    exchange.start()
    past = past + acc
    exchange.wait_recv()
    mine = full.at[shard(x, z), :]
    mine[...] = past + partner[...]

    near = sorted(range(1, NZ), key=lambda d: (far(d, NZ), d))
    outward = []

    def onto_x(n, at_z):
        block = full.at[shard(x, at_z), :]
        for i in range(1, nc):
            copy = pltpu.make_async_remote_copy(
                src_ref=block, dst_ref=block, send_sem=send_t.at[n, i - 1], recv_sem=recv_t.at[at_z, i - 1],
                device_id=(x_peer(i), gy), device_id_type=MESH,
            )
            copy.start()
            onward.append(copy)

    onward = []
    for k, turn in enumerate(near):
        copy = pltpu.make_async_remote_copy(
            src_ref=mine, dst_ref=mine, send_sem=send_s.at[k], recv_sem=recv_s.at[k],
            device_id=(z_peer(turn), gy), device_id_type=MESH,
        )
        copy.start()
        outward.append(copy)
    onto_x(0, z)
    for k, turn in enumerate(near):
        outward[k].wait_recv()
        onto_x(k + 1, ring(z, -turn, NZ))

    def arrived(at_z):
        for i in range(1, nc):
            block = full.at[shard(ring(x, -i, nc), at_z), :]
            pltpu.make_async_remote_copy(
                src_ref=block, dst_ref=block, send_sem=send_t.at[0, i - 1], recv_sem=recv_t.at[at_z, i - 1],
                device_id=(x_peer(i), gy), device_id_type=MESH,
            ).wait_recv()

    arrived(0)

    def ready():
        for at_z in range(1, NZ):
            arrived(at_z)

    factorize(blocks, full, ready, nc * cut, factor, answer)
    rows_out[...] = factor[pl.ds(pl.multiple_of(gx * rows, rows), rows), :]
    per = B // rows
    picked = answer[pl.ds(pl.multiple_of(8 * lax.div(gx, per), 8), 8), :]
    estimate_out[...] = pltpu.roll(picked, lax.rem(B - rows * lax.rem(gx, per), B), 1)[0:1, :rows]
    for copies in across:
        for copy in copies:
            copy.wait_send()
    for copy in along + [exchange] + outward + onward:
        copy.wait_send()

    @pl.loop(1, ny // 2 - y)
    def _(step):
        later(step).wait_send()


def gathered(nx, ny, tangent, well, live_from, noise_std, innovation, prior, prior_info):
    rows, obs = tangent.shape
    size = rows * nx
    packed = len(pairs(size // B)) * B
    cut = packed // nx
    nc = nx // NZ
    vmem = pltpu.VMEM
    hbm = pl.BlockSpec(memory_space=pltpu.HBM)
    dma = pltpu.SemaphoreType.DMA
    return pl.pallas_call(
        functools.partial(gather_kernel, nx, ny),
        out_shape=[
            jax.ShapeDtypeStruct((rows, size), jnp.float32),
            jax.ShapeDtypeStruct((1, rows), jnp.float32),
        ],
        in_specs=[hbm] * 7,
        out_specs=[pl.BlockSpec(memory_space=pltpu.VMEM)] * 2,
        scratch_shapes=[
            vmem((packed, B), jnp.float32),
            vmem((size, size), jnp.float32),
            vmem((8 * (size // B), B), jnp.float32),
            vmem((size, obs // nx), jnp.float32),
            vmem((packed, B), jnp.float32),
            vmem((NZ, nc - 1, cut, B), jnp.float32),
            vmem((NZ - 1, cut, B), jnp.float32),
            vmem((NZ - 1, cut, B), jnp.float32),
            vmem((ny // 2, cut, B), jnp.float32),
            vmem((cut, B), jnp.float32),
            vmem((cut, B), jnp.float32),
            vmem((cut, B), jnp.float32),
            vmem((8, B), jnp.int32),
            vmem((8, B), jnp.float32),
            vmem((rows, size), jnp.float32),
            pltpu.SMEM(live_from.shape, jnp.int32),
            pltpu.SMEM(noise_std.shape, jnp.float32),
            pltpu.SMEM(prior_info.shape, jnp.float32),
            dma((7,)),
            dma((nx - 1,)), dma((nx - 1,)),
            dma((NZ, nc - 1)), dma((NZ, nc - 1)),
            dma((NZ - 1,)), dma((NZ - 1,)),
            dma((ny // 2,)), dma((ny // 2,)),
            dma((NZ - 1,)), dma((NZ - 1,)),
            dma((NZ, nc - 1)), dma((NZ, nc - 1)),
        ],
        compiler_params=pltpu.CompilerParams(
            collective_id=0, has_side_effects=True, vmem_limit_bytes=56 * 2**20
        ),
        name="gather",
    )(tangent, well, live_from, noise_std, innovation, prior, prior_info)


def mm(a, b, dims):
    return lax.dot_general(
        a, b, (dims, ((), ())), precision=HIGHEST, preferred_element_type=jnp.float32
    )


NN = ((1,), (0,))
NT = ((1,), (1,))


def splat(row):
    return jnp.broadcast_to(row, (8, B))


def factor_block(s, width):
    tiles = width // 8
    sub = lax.broadcasted_iota(jnp.int32, (8, B), 0)
    lanes = lax.broadcasted_iota(jnp.int32, (B, B), 1)
    subs = lax.broadcasted_iota(jnp.int32, (B, B), 0)
    rest = jnp.concatenate([s, jnp.where(subs == lanes, 1.0, 0.0).astype(jnp.float32)], axis=1)
    done = []
    for lo in range(0, B, width):
        panel = [[rest[8 * t : 8 * t + 8, h * B : (h + 1) * B] for h in range(2)] for t in range(tiles)]
        pivots = [jnp.ones((8, B), jnp.float32) for _ in range(tiles)]

        def spread(g):
            at = lo + 8 * g
            return [
                [jnp.broadcast_to(panel[t][0][:, at + j : at + j + 1], (8, B)) if t >= g else None for t in range(tiles)]
                for j in range(8)
            ]

        columns = spread(0)
        for g in range(tiles):
            if g + 1 < tiles:
                columns = columns + spread(g + 1)
            for k in range(8 * g, 8 * g + 8, 2):
                r = k - 8 * g
                one, two = columns[k], columns[k + 1]
                a, b, c = splat(one[g][r : r + 1]), splat(one[g][r + 1 : r + 2]), splat(two[g][r + 1 : r + 2])
                det = a * c - b * b
                inverse, first = 1.0 / det, 1.0 / a
                pivots[g] = jnp.where(sub == r, a, jnp.where(sub == r + 1, det * first, pivots[g]))
                u = [(c * one[t] - b * two[t]) * inverse if t >= g else None for t in range(tiles)]
                v = [(a * two[t] - b * one[t]) * inverse if t >= g else None for t in range(tiles)]
                for j in range(k + 2, len(columns)):
                    tj, rj = divmod(j, 8)
                    p, q = splat(u[tj][rj : rj + 1]), splat(v[tj][rj : rj + 1])
                    for t in range(tj, tiles):
                        columns[j][t] = columns[j][t] - (one[t] * p + two[t] * q)
                u[g] = jnp.where(sub > r + 1, u[g], jnp.where(sub == r + 1, b * first, 0.0))
                v[g] = jnp.where(sub > r + 1, v[g], 0.0)
                for h in range(2):
                    p, q = splat(panel[g][h][r : r + 1]), splat(panel[g][h][r + 1 : r + 2])
                    for t in range(g, tiles):
                        panel[t][h] = panel[t][h] - (u[t] * p + v[t] * q)
        rows = jnp.concatenate(
            [
                jnp.concatenate([panel[t][h] * lax.rsqrt(pivots[t]) for h in range(2)], axis=1)
                for t in range(tiles)
            ],
            axis=0,
        )
        done.append(rows)
        if lo + width < B:
            left = jnp.transpose(rows[:, :B])[lo + width :]
            rest = rest[width:] - mm(left, rows, NN)
    both = jnp.concatenate(done, axis=0)
    return jnp.where(subs <= lanes, both[:, :B], 0.0), both[:, B:]


def factorize(blocks, packed, ready, first, factor, answer):
    lanes = lax.broadcasted_iota(jnp.int32, (B, B), 1)
    subs = lax.broadcasted_iota(jnp.int32, (B, B), 0)
    lane = lax.broadcasted_iota(jnp.int32, (8, B), 1)
    s, vector = {}, []

    def take(k, i, j):
        tile = packed[k * B : (k + 1) * B, :]
        if i == j:
            vector.append(jnp.where(lane == B - 1, splat(tile[B - 2 : B - 1, 0:1]), splat(tile[B - 1 : B, :])))
            tile = jnp.where(subs <= lanes, tile, jnp.transpose(jnp.where(subs < lanes, tile, 0.0)))
        s[i, j] = tile

    assert first >= B
    take(0, 0, 0)
    factor[...] = jnp.zeros_like(factor)
    forward, inverse, right = [], [], {}
    for i in range(blocks):
        lo, hi = i * B, (i + 1) * B
        r, t = factor_block(s[i, i], 32)
        factor[lo:hi, lo:hi] = r
        inverse.append(t)
        forward.append(mm(vector[i], t, NT))
        if i == 0:
            ready()
            for k, (p, q) in enumerate(pairs(blocks)):
                if k:
                    take(k, p, q)
        if i + 1 < blocks:
            strip = mm(t, jnp.concatenate([s[i, j] for j in range(i + 1, blocks)], axis=1), NN)
            factor[lo:hi, hi:] = strip
            for j in range(i + 1, blocks):
                at = (j - i - 1) * B
                right[i, j] = strip[:, at : at + B]
                update = mm(jnp.transpose(right[i, j]), strip[:, at:], NN)
                for k in range(j, blocks):
                    s[j, k] = s[j, k] - update[:, (k - j) * B : (k - j + 1) * B]
            update = mm(forward[i], strip, NN)
            for j in range(i + 1, blocks):
                vector[j] = vector[j] - update[:, (j - i - 1) * B : (j - i) * B]
    x = [None] * blocks
    for i in reversed(range(blocks)):
        z = forward[i]
        for j in range(i + 1, blocks):
            z = z - mm(x[j], right[i, j], NT)
        x[i] = mm(z, inverse[i], NN)
        answer[8 * i : 8 * i + 8, :] = x[i]


def body(nx, ny, tangent, well_of_obs, live_from, noise_std, innovation, prior_factor, prior_info):
    factor_rows, estimate_part = gathered(
        nx, ny, tangent, well_of_obs.reshape(-1, B), live_from, noise_std,
        innovation.reshape(-1, B), prior_factor, prior_info,
    )
    return (factor_rows[None, :, :], estimate_part)


def solution(mesh):
    in_specs = (P("gx", "gy"), P("gy"), P(), P(), P("gy"), P("gx", None), P())
    out_specs = (P("gy", "gx", None), P("gy", "gx"))
    nx, ny = mesh.shape["gx"], mesh.shape["gy"]
    return jax.shard_map(
        functools.partial(body, nx, ny), mesh=mesh, in_specs=in_specs, out_specs=out_specs, check_vma=False
    )
```

```python
import functools

import jax
import jax.numpy as jnp
from jax import lax
from jax.experimental import pallas as pl
from jax.experimental.pallas import tpu as pltpu
from jax.sharding import PartitionSpec as P

MESH = pl.DeviceIdType.MESH
HIGHEST = lax.Precision.HIGHEST
B = 128


def pairs(blocks):
    return [(i, j) for i in range(blocks) for j in range(i, blocks)]


def nt(a, b):
    return lax.dot_general(
        a, b, (((1,), (1,)), ((), ())), precision=HIGHEST, preferred_element_type=jnp.float32
    )


def pieces(v):
    a = v.astype(jnp.bfloat16)
    rest = v - a.astype(jnp.float32)
    b = rest.astype(jnp.bfloat16)
    return a, b, (rest - b.astype(jnp.float32)).astype(jnp.bfloat16)


def left_of(v):
    a, b, c = pieces(v)
    return jnp.concatenate([a, a, b, a, c, b], axis=1)


def right_of(v):
    a, b, c = pieces(v)
    return jnp.concatenate([a, b, a, c, a, b], axis=1)


def nt_pieces(a, b):
    return lax.dot_general(a, b, (((1,), (1,)), ((), ())), preferred_element_type=jnp.float32)


NZ = 8


def gather_kernel(
    nx, ny,
    tangent, well, live_from, noise_std, innovation, prior, prior_info,
    rows_out, estimate_out,
    full, factor, answer,
    got, part, from_x, sums, from_z, earlier, total, passed, partner,
    well_v, innovation_v, prior_v, live_s, noise_s, info_s,
    in_sem, send_a, recv_a, send_x, recv_x, send_z, recv_z, send_y, recv_y, send_s, recv_s, send_t, recv_t,
):
    gx, gy = lax.axis_index("gx"), lax.axis_index("gy")
    x, z = lax.div(gx, NZ), lax.rem(gx, NZ)
    nc = nx // NZ
    rows, obs = tangent.shape
    size = rows * nx
    share = obs // nx
    blocks = size // B
    halves = share // B
    cut = part.shape[0] // nx

    def ring(at, by, n):
        return lax.rem(at + by + n, n)

    def x_peer(by):
        return ring(x, by, nc) * NZ + z

    def z_peer(by):
        return x * NZ + ring(z, by, NZ)

    def far(by, n):
        return min(by, n - by)

    hops = sorted(
        [(i, j) for i in range(nc) for j in range(NZ) if i or j],
        key=lambda d: (-far(d[1], NZ), -far(d[0], nc), d),
    )
    turns = sorted(range(1, NZ), key=lambda d: (-far(d, NZ), d))

    group = 8 // halves
    tile = pl.ds(pl.multiple_of(8 * lax.div(gx, group), 8), 8)
    loads = [
        pltpu.make_async_copy(src, dst, in_sem.at[k])
        for k, (src, dst) in enumerate(
            [
                (well.at[tile, :], well_v), (innovation.at[tile, :], innovation_v), (prior, prior_v),
                (live_from, live_s), (noise_std, noise_s), (prior_info, info_s),
            ]
        )
    ]
    for load in loads:
        load.start()

    def piece(peer):
        return tangent.at[:, pl.ds(pl.multiple_of(peer * share, share), share)]

    def slot(owner):
        return got.at[pl.ds(pl.multiple_of(owner * rows, rows), rows), :]

    own = pltpu.make_async_copy(piece(gx), slot(gx), in_sem.at[6])
    own.start()

    barrier = pltpu.get_barrier_semaphore()
    for i, j in hops:
        pl.semaphore_signal(
            barrier, inc=1, device_id=(ring(x, i, nc) * NZ + ring(z, j, NZ), gy), device_id_type=MESH
        )
    core = lax.rem(gy, 2)
    other = gy + 1 - 2 * core
    for step in range(2, ny, 2):
        pl.semaphore_signal(barrier, inc=1, device_id=(gx, ring(gy, step, ny)), device_id_type=MESH)
    pl.semaphore_signal(barrier, inc=1, device_id=(gx, other), device_id_type=MESH)
    pl.semaphore_wait(barrier, nx - 1 + ny // 2)

    swaps = []
    for k, (i, j) in enumerate(hops):
        peer = ring(x, i, nc) * NZ + ring(z, j, NZ)
        copy = pltpu.make_async_remote_copy(
            src_ref=piece(peer), dst_ref=slot(gx), send_sem=send_a.at[k], recv_sem=recv_a.at[k],
            device_id=(peer, gy), device_id_type=MESH,
        )
        copy.start()
        swaps.append(copy)

    for load in loads:
        load.wait()
    at = halves * lax.rem(gx, group)
    wells = well_v[pl.ds(at, halves), :]
    row_index = (
        gy * obs + gx * share
        + B * lax.broadcasted_iota(jnp.int32, (halves, B), 0)
        + lax.broadcasted_iota(jnp.int32, (halves, B), 1)
    )
    starts = jnp.zeros((halves, B), jnp.int32)
    noise = jnp.ones((halves, B), jnp.float32)
    for k in range(live_from.shape[0]):
        here = wells == k
        starts = jnp.where(here, live_s[k], starts)
        noise = jnp.where(here, noise_s[k], noise)
    weight = jnp.where(row_index >= starts, 1.0 / noise, 0.0)
    scaled = weight * innovation_v[pl.ds(at, halves), :]

    first = jnp.where(gy == 0, 1.0, 0.0).astype(jnp.float32)
    moment = jnp.zeros((1, size), jnp.float32)
    for k in range(rows):
        moment = moment + info_s[gx * rows + k] * prior_v[k : k + 1, :]
    moment = first * moment
    prior_t = first * jnp.transpose(prior_v[...])
    starts_at = {}
    row = 0
    for i in range(blocks):
        strip = nt(prior_t[i * B : (i + 1) * B], prior_t[i * B :])
        for j in range(i, blocks):
            part[row : row + B, :] = strip[:, (j - i) * B : (j - i + 1) * B]
            starts_at[i, j] = row
            row += B
    scaled = left_of(jnp.concatenate([jnp.broadcast_to(scaled[h : h + 1, :], (16, B)) for h in range(halves)], axis=1))

    own.wait()
    for copy in swaps:
        copy.wait()

    whitened = jnp.concatenate([got[:, h * B : (h + 1) * B] * weight[h : h + 1, :] for h in range(halves)], axis=1)
    left, right = left_of(whitened), right_of(whitened)
    moment = moment + nt_pieces(scaled, right)[0:1, :]
    lanes = lax.broadcasted_iota(jnp.int32, (B, B), 1)
    subs = lax.broadcasted_iota(jnp.int32, (B, B), 0)
    for i in range(blocks):
        lo = i * B
        strip = nt_pieces(left[lo : lo + B], right[lo:])
        for j in range(i, blocks):
            row = starts_at[i, j]
            block = part[row : row + B, :] + strip[:, (j - i) * B : (j - i + 1) * B]
            if i == j:
                vector = moment[:, lo : lo + B]
                last = vector[:, B - 1 : B]
                block = jnp.where(subs > lanes, jnp.where(subs == B - 1, vector, last), block)
            part[row : row + B, :] = block

    def shard(at_x, at_z):
        return pl.ds(pl.multiple_of((at_z * nc + at_x) * cut, 8), cut)

    order = turns + [0]
    across = []
    for k, turn in enumerate(order):
        across.append([])
        for i in range(1, nc):
            copy = pltpu.make_async_remote_copy(
                src_ref=part.at[shard(ring(x, i, nc), ring(z, turn, NZ)), :], dst_ref=from_x.at[k, i - 1],
                send_sem=send_x.at[k, i - 1], recv_sem=recv_x.at[k, i - 1],
                device_id=(x_peer(i), gy), device_id_type=MESH,
            )
            copy.start()
            across[k].append(copy)
    along = []
    for k, turn in enumerate(order):
        acc = part[shard(x, ring(z, turn, NZ)), :]
        for i in range(1, nc):
            across[k][i - 1].wait_recv()
            acc = acc + from_x[k, i - 1]
        if turn:
            sums[k] = acc
            copy = pltpu.make_async_remote_copy(
                src_ref=sums.at[k], dst_ref=from_z.at[k], send_sem=send_z.at[k], recv_sem=recv_z.at[k],
                device_id=(z_peer(turn), gy), device_id_type=MESH,
            )
            copy.start()
            along.append(copy)
    for k, copy in enumerate(along):
        copy.wait_recv()
        acc = acc + from_z[k]
    total[...] = acc

    y = lax.div(gy, 2)

    def later(step):
        return pltpu.make_async_remote_copy(
            src_ref=total, dst_ref=earlier.at[step],
            send_sem=send_y.at[step], recv_sem=recv_y.at[step],
            device_id=(gx, ring(gy, 2 * step, ny)), device_id_type=MESH,
        )

    @pl.loop(1, ny // 2 - y)
    def _(step):
        later(step).start()

    def before(step, sum_):
        later(step).wait_recv()
        return sum_ + earlier[step]

    past = lax.fori_loop(1, y + 1, before, jnp.zeros_like(acc))
    passed[...] = jnp.where(core == 0, past + acc, past)
    exchange = pltpu.make_async_remote_copy(
        src_ref=passed, dst_ref=partner, send_sem=send_y.at[0], recv_sem=recv_y.at[0],
        device_id=(gx, other), device_id_type=MESH,
    )
    exchange.start()
    past = past + acc
    exchange.wait_recv()
    mine = full.at[shard(x, z), :]
    mine[...] = past + partner[...]

    near = sorted(range(1, NZ), key=lambda d: (far(d, NZ), d))
    outward = []

    def onto_x(n, at_z):
        block = full.at[shard(x, at_z), :]
        for i in range(1, nc):
            copy = pltpu.make_async_remote_copy(
                src_ref=block, dst_ref=block, send_sem=send_t.at[n, i - 1], recv_sem=recv_t.at[at_z, i - 1],
                device_id=(x_peer(i), gy), device_id_type=MESH,
            )
            copy.start()
            onward.append(copy)

    onward = []
    for k, turn in enumerate(near):
        copy = pltpu.make_async_remote_copy(
            src_ref=mine, dst_ref=mine, send_sem=send_s.at[k], recv_sem=recv_s.at[k],
            device_id=(z_peer(turn), gy), device_id_type=MESH,
        )
        copy.start()
        outward.append(copy)
    onto_x(0, z)
    for k, turn in enumerate(near):
        outward[k].wait_recv()
        onto_x(k + 1, ring(z, -turn, NZ))

    def arrived(at_z):
        for i in range(1, nc):
            block = full.at[shard(ring(x, -i, nc), at_z), :]
            pltpu.make_async_remote_copy(
                src_ref=block, dst_ref=block, send_sem=send_t.at[0, i - 1], recv_sem=recv_t.at[at_z, i - 1],
                device_id=(x_peer(i), gy), device_id_type=MESH,
            ).wait_recv()

    arrived(0)

    def ready():
        for at_z in range(1, NZ):
            arrived(at_z)

    factorize(blocks, full, ready, nc * cut, factor, answer)
    rows_out[...] = factor[pl.ds(pl.multiple_of(gx * rows, rows), rows), :]
    per = B // rows
    picked = answer[pl.ds(pl.multiple_of(8 * lax.div(gx, per), 8), 8), :]
    estimate_out[...] = pltpu.roll(picked, lax.rem(B - rows * lax.rem(gx, per), B), 1)[0:1, :rows]
    for copies in across:
        for copy in copies:
            copy.wait_send()
    for copy in along + [exchange] + outward + onward:
        copy.wait_send()

    @pl.loop(1, ny // 2 - y)
    def _(step):
        later(step).wait_send()


def gathered(nx, ny, tangent, well, live_from, noise_std, innovation, prior, prior_info):
    rows, obs = tangent.shape
    size = rows * nx
    packed = len(pairs(size // B)) * B
    cut = packed // nx
    nc = nx // NZ
    vmem = pltpu.VMEM
    hbm = pl.BlockSpec(memory_space=pltpu.HBM)
    dma = pltpu.SemaphoreType.DMA
    return pl.pallas_call(
        functools.partial(gather_kernel, nx, ny),
        out_shape=[
            jax.ShapeDtypeStruct((rows, size), jnp.float32),
            jax.ShapeDtypeStruct((1, rows), jnp.float32),
        ],
        in_specs=[hbm] * 7,
        out_specs=[pl.BlockSpec(memory_space=pltpu.VMEM)] * 2,
        scratch_shapes=[
            vmem((packed, B), jnp.float32),
            vmem((size, size), jnp.float32),
            vmem((8 * (size // B), B), jnp.float32),
            vmem((size, obs // nx), jnp.float32),
            vmem((packed, B), jnp.float32),
            vmem((NZ, nc - 1, cut, B), jnp.float32),
            vmem((NZ - 1, cut, B), jnp.float32),
            vmem((NZ - 1, cut, B), jnp.float32),
            vmem((ny // 2, cut, B), jnp.float32),
            vmem((cut, B), jnp.float32),
            vmem((cut, B), jnp.float32),
            vmem((cut, B), jnp.float32),
            vmem((8, B), jnp.int32),
            vmem((8, B), jnp.float32),
            vmem((rows, size), jnp.float32),
            pltpu.SMEM(live_from.shape, jnp.int32),
            pltpu.SMEM(noise_std.shape, jnp.float32),
            pltpu.SMEM(prior_info.shape, jnp.float32),
            dma((7,)),
            dma((nx - 1,)), dma((nx - 1,)),
            dma((NZ, nc - 1)), dma((NZ, nc - 1)),
            dma((NZ - 1,)), dma((NZ - 1,)),
            dma((ny // 2,)), dma((ny // 2,)),
            dma((NZ - 1,)), dma((NZ - 1,)),
            dma((NZ, nc - 1)), dma((NZ, nc - 1)),
        ],
        compiler_params=pltpu.CompilerParams(
            collective_id=0, has_side_effects=True, vmem_limit_bytes=56 * 2**20
        ),
        name="gather",
    )(tangent, well, live_from, noise_std, innovation, prior, prior_info)


def mm(a, b, dims):
    return lax.dot_general(
        stack(a, LEFT, dims[0][0]), stack(b, RIGHT, dims[1][0]), (dims, ((), ())), preferred_element_type=jnp.float32
    )


NN = ((1,), (0,))
NT = ((1,), (1,))


def stack(v, order, axis):
    parts = pieces(v)
    return jnp.concatenate([parts[k] for k in order], axis=axis)


LEFT, RIGHT = (0, 0, 1, 0, 2, 1), (0, 1, 0, 2, 0, 1)


def tn_pieces(a, b):
    return lax.dot_general(
        stack(a, LEFT, 0), stack(b, RIGHT, 0), (((0,), (0,)), ((), ())), preferred_element_type=jnp.float32
    )


def splat(row):
    return jnp.broadcast_to(row, (8, B))


def factor_block(s, width):
    tiles = width // 8
    sub = lax.broadcasted_iota(jnp.int32, (8, B), 0)
    lanes = lax.broadcasted_iota(jnp.int32, (B, B), 1)
    subs = lax.broadcasted_iota(jnp.int32, (B, B), 0)
    rest = jnp.concatenate([s, jnp.where(subs == lanes, 1.0, 0.0).astype(jnp.float32)], axis=1)
    done = []
    for lo in range(0, B, width):
        panel = [[rest[8 * t : 8 * t + 8, h * B : (h + 1) * B] for h in range(2)] for t in range(tiles)]
        pivots = [jnp.ones((8, B), jnp.float32) for _ in range(tiles)]

        def spread(g):
            at = lo + 8 * g
            return [
                [jnp.broadcast_to(panel[t][0][:, at + j : at + j + 1], (8, B)) if t >= g else None for t in range(tiles)]
                for j in range(8)
            ]

        columns = spread(0)
        for g in range(tiles):
            if g + 1 < tiles:
                columns = columns + spread(g + 1)
            for k in range(8 * g, 8 * g + 8, 2):
                r = k - 8 * g
                one, two = columns[k], columns[k + 1]
                a, b, c = splat(one[g][r : r + 1]), splat(one[g][r + 1 : r + 2]), splat(two[g][r + 1 : r + 2])
                det = a * c - b * b
                inverse, first = 1.0 / det, 1.0 / a
                pivots[g] = jnp.where(sub == r, a, jnp.where(sub == r + 1, det * first, pivots[g]))
                u = [(c * one[t] - b * two[t]) * inverse if t >= g else None for t in range(tiles)]
                v = [(a * two[t] - b * one[t]) * inverse if t >= g else None for t in range(tiles)]
                for j in range(k + 2, len(columns)):
                    tj, rj = divmod(j, 8)
                    p, q = splat(u[tj][rj : rj + 1]), splat(v[tj][rj : rj + 1])
                    for t in range(tj, tiles):
                        columns[j][t] = columns[j][t] - (one[t] * p + two[t] * q)
                u[g] = jnp.where(sub > r + 1, u[g], jnp.where(sub == r + 1, b * first, 0.0))
                v[g] = jnp.where(sub > r + 1, v[g], 0.0)
                for h in range(2):
                    p, q = splat(panel[g][h][r : r + 1]), splat(panel[g][h][r + 1 : r + 2])
                    for t in range(g, tiles):
                        panel[t][h] = panel[t][h] - (u[t] * p + v[t] * q)
        rows = jnp.concatenate(
            [
                jnp.concatenate([panel[t][h] * lax.rsqrt(pivots[t]) for h in range(2)], axis=1)
                for t in range(tiles)
            ],
            axis=0,
        )
        done.append(rows)
        if lo + width < B:
            rest = rest[width:] - tn_pieces(rows[:, :B], rows)[lo + width :]
    both = jnp.concatenate(done, axis=0)
    return jnp.where(subs <= lanes, both[:, :B], 0.0), both[:, B:]


def factorize(blocks, packed, ready, first, factor, answer):
    lanes = lax.broadcasted_iota(jnp.int32, (B, B), 1)
    subs = lax.broadcasted_iota(jnp.int32, (B, B), 0)
    lane = lax.broadcasted_iota(jnp.int32, (16, B), 1)
    s, vector = {}, []

    def take(k, i, j):
        tile = packed[k * B : (k + 1) * B, :]
        if i == j:
            vector.append(jnp.where(lane == B - 1, jnp.broadcast_to(tile[B - 2 : B - 1, 0:1], (16, B)), jnp.broadcast_to(tile[B - 1 : B, :], (16, B))))
            tile = jnp.where(subs <= lanes, tile, jnp.transpose(jnp.where(subs < lanes, tile, 0.0)))
        s[i, j] = tile

    assert first >= B
    take(0, 0, 0)
    factor[...] = jnp.zeros_like(factor)
    forward, inverse, right = [], [], {}
    for i in range(blocks):
        lo, hi = i * B, (i + 1) * B
        r, t = factor_block(s[i, i], 32)
        factor[lo:hi, lo:hi] = r
        inverse.append(t)
        forward.append(mm(vector[i], t, NT))
        if i == 0:
            ready()
            for k, (p, q) in enumerate(pairs(blocks)):
                if k:
                    take(k, p, q)
        if i + 1 < blocks:
            strip = mm(t, jnp.concatenate([s[i, j] for j in range(i + 1, blocks)], axis=1), NN)
            factor[lo:hi, hi:] = strip
            for j in range(i + 1, blocks):
                at = (j - i - 1) * B
                right[i, j] = strip[:, at : at + B]
                update = mm(jnp.transpose(right[i, j]), strip[:, at:], NN)
                for k in range(j, blocks):
                    s[j, k] = s[j, k] - update[:, (k - j) * B : (k - j + 1) * B]
            update = mm(forward[i], strip, NN)
            for j in range(i + 1, blocks):
                vector[j] = vector[j] - update[:, (j - i - 1) * B : (j - i) * B]
    x = [None] * blocks
    for i in reversed(range(blocks)):
        z = forward[i]
        for j in range(i + 1, blocks):
            z = z - mm(x[j], right[i, j], NT)
        x[i] = mm(z, inverse[i], NN)
        answer[8 * i : 8 * i + 8, :] = x[i][:8]


def body(nx, ny, tangent, well_of_obs, live_from, noise_std, innovation, prior_factor, prior_info):
    factor_rows, estimate_part = gathered(
        nx, ny, tangent, well_of_obs.reshape(-1, B), live_from, noise_std,
        innovation.reshape(-1, B), prior_factor, prior_info,
    )
    return (factor_rows[None, :, :], estimate_part)


def solution(mesh):
    in_specs = (P("gx", "gy"), P("gy"), P(), P(), P("gy"), P("gx", None), P())
    out_specs = (P("gy", "gx", None), P("gy", "gx"))
    nx, ny = mesh.shape["gx"], mesh.shape["gy"]
    return jax.shard_map(
        functools.partial(body, nx, ny), mesh=mesh, in_specs=in_specs, out_specs=out_specs, check_vma=False
    )
```

```python
import functools

import jax
import jax.numpy as jnp
from jax import lax
from jax.experimental import pallas as pl
from jax.experimental.pallas import tpu as pltpu
from jax.sharding import PartitionSpec as P

MESH = pl.DeviceIdType.MESH
HIGHEST = lax.Precision.HIGHEST
B = 128


def pairs(blocks):
    return [(i, j) for i in range(blocks) for j in range(i, blocks)]


def nt(a, b):
    return lax.dot_general(
        a, b, (((1,), (1,)), ((), ())), precision=HIGHEST, preferred_element_type=jnp.float32
    )


def pieces(v):
    a = v.astype(jnp.bfloat16)
    rest = v - a.astype(jnp.float32)
    b = rest.astype(jnp.bfloat16)
    return a, b, (rest - b.astype(jnp.float32)).astype(jnp.bfloat16)


def left_of(v):
    a, b, c = pieces(v)
    return jnp.concatenate([a, a, b, a, c, b], axis=1)


def right_of(v):
    a, b, c = pieces(v)
    return jnp.concatenate([a, b, a, c, a, b], axis=1)


def nt_pieces(a, b):
    return lax.dot_general(a, b, (((1,), (1,)), ((), ())), preferred_element_type=jnp.float32)


NZ = 8


def gather_kernel(
    nx, ny,
    tangent, well, live_from, noise_std, innovation, prior, prior_info,
    rows_out, estimate_out,
    full, factor, answer,
    got, part, from_x, sums, from_z, earlier, total, passed, partner,
    well_v, innovation_v, prior_v, live_s, noise_s, info_s,
    in_sem, send_a, recv_a, send_x, recv_x, send_z, recv_z, send_y, recv_y, send_s, recv_s, send_t, recv_t,
):
    gx, gy = lax.axis_index("gx"), lax.axis_index("gy")
    x, z = lax.div(gx, NZ), lax.rem(gx, NZ)
    nc = nx // NZ
    rows, obs = tangent.shape
    size = rows * nx
    share = obs // nx
    blocks = size // B
    halves = share // B
    cut = part.shape[0] // nx

    def ring(at, by, n):
        return lax.rem(at + by + n, n)

    def x_peer(by):
        return ring(x, by, nc) * NZ + z

    def z_peer(by):
        return x * NZ + ring(z, by, NZ)

    def far(by, n):
        return min(by, n - by)

    hops = sorted(
        [(i, j) for i in range(nc) for j in range(NZ) if i or j],
        key=lambda d: (-far(d[1], NZ), -far(d[0], nc), d),
    )
    turns = sorted(range(1, NZ), key=lambda d: (-far(d, NZ), d))

    group = 8 // halves
    tile = pl.ds(pl.multiple_of(8 * lax.div(gx, group), 8), 8)
    loads = [
        pltpu.make_async_copy(src, dst, in_sem.at[k])
        for k, (src, dst) in enumerate(
            [
                (well.at[tile, :], well_v), (innovation.at[tile, :], innovation_v), (prior, prior_v),
                (live_from, live_s), (noise_std, noise_s), (prior_info, info_s),
            ]
        )
    ]
    for load in loads:
        load.start()

    def piece(peer):
        return tangent.at[:, pl.ds(pl.multiple_of(peer * share, share), share)]

    def slot(owner):
        return got.at[pl.ds(pl.multiple_of(owner * rows, rows), rows), :]

    own = pltpu.make_async_copy(piece(gx), slot(gx), in_sem.at[6])
    own.start()

    barrier = pltpu.get_barrier_semaphore()
    for i, j in hops:
        pl.semaphore_signal(
            barrier, inc=1, device_id=(ring(x, i, nc) * NZ + ring(z, j, NZ), gy), device_id_type=MESH
        )
    core = lax.rem(gy, 2)
    other = gy + 1 - 2 * core
    for step in range(2, ny, 2):
        pl.semaphore_signal(barrier, inc=1, device_id=(gx, ring(gy, step, ny)), device_id_type=MESH)
    pl.semaphore_signal(barrier, inc=1, device_id=(gx, other), device_id_type=MESH)
    pl.semaphore_wait(barrier, nx - 1 + ny // 2)

    swaps = []
    for k, (i, j) in enumerate(hops):
        peer = ring(x, i, nc) * NZ + ring(z, j, NZ)
        copy = pltpu.make_async_remote_copy(
            src_ref=piece(peer), dst_ref=slot(gx), send_sem=send_a.at[k], recv_sem=recv_a.at[k],
            device_id=(peer, gy), device_id_type=MESH,
        )
        copy.start()
        swaps.append(copy)

    for load in loads:
        load.wait()
    at = halves * lax.rem(gx, group)
    wells = well_v[pl.ds(at, halves), :]
    row_index = (
        gy * obs + gx * share
        + B * lax.broadcasted_iota(jnp.int32, (halves, B), 0)
        + lax.broadcasted_iota(jnp.int32, (halves, B), 1)
    )
    starts = jnp.zeros((halves, B), jnp.int32)
    noise = jnp.ones((halves, B), jnp.float32)
    for k in range(live_from.shape[0]):
        here = wells == k
        starts = jnp.where(here, live_s[k], starts)
        noise = jnp.where(here, noise_s[k], noise)
    weight = jnp.where(row_index >= starts, 1.0 / noise, 0.0)
    scaled = weight * innovation_v[pl.ds(at, halves), :]

    first = jnp.where(gy == 0, 1.0, 0.0).astype(jnp.float32)
    moment = jnp.zeros((1, size), jnp.float32)
    for k in range(rows):
        moment = moment + info_s[gx * rows + k] * prior_v[k : k + 1, :]
    moment = first * moment
    prior_t = first * jnp.transpose(prior_v[...])
    starts_at = {}
    row = 0
    for i in range(blocks):
        strip = nt(prior_t[i * B : (i + 1) * B], prior_t[i * B :])
        for j in range(i, blocks):
            part[row : row + B, :] = strip[:, (j - i) * B : (j - i + 1) * B]
            starts_at[i, j] = row
            row += B
    scaled = left_of(jnp.concatenate([jnp.broadcast_to(scaled[h : h + 1, :], (16, B)) for h in range(halves)], axis=1))

    own.wait()
    for copy in swaps:
        copy.wait()

    whitened = jnp.concatenate([got[:, h * B : (h + 1) * B] * weight[h : h + 1, :] for h in range(halves)], axis=1)
    left, right = left_of(whitened), right_of(whitened)
    moment = moment + nt_pieces(scaled, right)[0:1, :]
    lanes = lax.broadcasted_iota(jnp.int32, (B, B), 1)
    subs = lax.broadcasted_iota(jnp.int32, (B, B), 0)
    for i in range(blocks):
        lo = i * B
        strip = nt_pieces(left[lo : lo + B], right[lo:])
        for j in range(i, blocks):
            row = starts_at[i, j]
            block = part[row : row + B, :] + strip[:, (j - i) * B : (j - i + 1) * B]
            if i == j:
                vector = moment[:, lo : lo + B]
                last = vector[:, B - 1 : B]
                block = jnp.where(subs > lanes, jnp.where(subs == B - 1, vector, last), block)
            part[row : row + B, :] = block

    def shard(at_x, at_z):
        return pl.ds(pl.multiple_of((at_z * nc + at_x) * cut, 8), cut)

    order = turns + [0]
    across = []
    for k, turn in enumerate(order):
        across.append([])
        for i in range(1, nc):
            copy = pltpu.make_async_remote_copy(
                src_ref=part.at[shard(ring(x, i, nc), ring(z, turn, NZ)), :], dst_ref=from_x.at[k, i - 1],
                send_sem=send_x.at[k, i - 1], recv_sem=recv_x.at[k, i - 1],
                device_id=(x_peer(i), gy), device_id_type=MESH,
            )
            copy.start()
            across[k].append(copy)
    along = []
    for k, turn in enumerate(order):
        acc = part[shard(x, ring(z, turn, NZ)), :]
        for i in range(1, nc):
            across[k][i - 1].wait_recv()
            acc = acc + from_x[k, i - 1]
        if turn:
            sums[k] = acc
            copy = pltpu.make_async_remote_copy(
                src_ref=sums.at[k], dst_ref=from_z.at[k], send_sem=send_z.at[k], recv_sem=recv_z.at[k],
                device_id=(z_peer(turn), gy), device_id_type=MESH,
            )
            copy.start()
            along.append(copy)
    for k, copy in enumerate(along):
        copy.wait_recv()
        acc = acc + from_z[k]
    total[...] = acc

    y = lax.div(gy, 2)

    def later(step):
        return pltpu.make_async_remote_copy(
            src_ref=total, dst_ref=earlier.at[step],
            send_sem=send_y.at[step], recv_sem=recv_y.at[step],
            device_id=(gx, ring(gy, 2 * step, ny)), device_id_type=MESH,
        )

    @pl.loop(1, ny // 2 - y)
    def _(step):
        later(step).start()

    def before(step, sum_):
        later(step).wait_recv()
        return sum_ + earlier[step]

    past = lax.fori_loop(1, y + 1, before, jnp.zeros_like(acc))
    passed[...] = jnp.where(core == 0, past + acc, past)
    exchange = pltpu.make_async_remote_copy(
        src_ref=passed, dst_ref=partner, send_sem=send_y.at[0], recv_sem=recv_y.at[0],
        device_id=(gx, other), device_id_type=MESH,
    )
    exchange.start()
    past = past + acc
    exchange.wait_recv()
    mine = full.at[shard(x, z), :]
    mine[...] = past + partner[...]

    near = sorted(range(1, NZ), key=lambda d: (far(d, NZ), d))
    outward = []

    def onto_x(n, at_z):
        block = full.at[shard(x, at_z), :]
        for i in range(1, nc):
            copy = pltpu.make_async_remote_copy(
                src_ref=block, dst_ref=block, send_sem=send_t.at[n, i - 1], recv_sem=recv_t.at[at_z, i - 1],
                device_id=(x_peer(i), gy), device_id_type=MESH,
            )
            copy.start()
            onward.append(copy)

    onward = []
    for k, turn in enumerate(near):
        copy = pltpu.make_async_remote_copy(
            src_ref=mine, dst_ref=mine, send_sem=send_s.at[k], recv_sem=recv_s.at[k],
            device_id=(z_peer(turn), gy), device_id_type=MESH,
        )
        copy.start()
        outward.append(copy)
    onto_x(0, z)
    for k, turn in enumerate(near):
        outward[k].wait_recv()
        onto_x(k + 1, ring(z, -turn, NZ))

    def arrived(at_z):
        for i in range(1, nc):
            block = full.at[shard(ring(x, -i, nc), at_z), :]
            pltpu.make_async_remote_copy(
                src_ref=block, dst_ref=block, send_sem=send_t.at[0, i - 1], recv_sem=recv_t.at[at_z, i - 1],
                device_id=(x_peer(i), gy), device_id_type=MESH,
            ).wait_recv()

    arrived(0)

    left_out = list(range(1, NZ))

    def ready(upto):
        while left_out and left_out[0] * nc * cut < upto:
            arrived(left_out.pop(0))

    factorize(blocks, full, ready, nc * cut, factor, answer)
    rows_out[...] = factor[pl.ds(pl.multiple_of(gx * rows, rows), rows), :]
    per = B // rows
    picked = answer[pl.ds(pl.multiple_of(8 * lax.div(gx, per), 8), 8), :]
    estimate_out[...] = pltpu.roll(picked, lax.rem(B - rows * lax.rem(gx, per), B), 1)[0:1, :rows]
    for copies in across:
        for copy in copies:
            copy.wait_send()
    for copy in along + [exchange] + outward + onward:
        copy.wait_send()

    @pl.loop(1, ny // 2 - y)
    def _(step):
        later(step).wait_send()


def gathered(nx, ny, tangent, well, live_from, noise_std, innovation, prior, prior_info):
    rows, obs = tangent.shape
    size = rows * nx
    packed = len(pairs(size // B)) * B
    cut = packed // nx
    nc = nx // NZ
    vmem = pltpu.VMEM
    hbm = pl.BlockSpec(memory_space=pltpu.HBM)
    dma = pltpu.SemaphoreType.DMA
    return pl.pallas_call(
        functools.partial(gather_kernel, nx, ny),
        out_shape=[
            jax.ShapeDtypeStruct((rows, size), jnp.float32),
            jax.ShapeDtypeStruct((1, rows), jnp.float32),
        ],
        in_specs=[hbm] * 7,
        out_specs=[pl.BlockSpec(memory_space=pltpu.VMEM)] * 2,
        scratch_shapes=[
            vmem((packed, B), jnp.float32),
            vmem((size, size), jnp.float32),
            vmem((8 * (size // B), B), jnp.float32),
            vmem((size, obs // nx), jnp.float32),
            vmem((packed, B), jnp.float32),
            vmem((NZ, nc - 1, cut, B), jnp.float32),
            vmem((NZ - 1, cut, B), jnp.float32),
            vmem((NZ - 1, cut, B), jnp.float32),
            vmem((ny // 2, cut, B), jnp.float32),
            vmem((cut, B), jnp.float32),
            vmem((cut, B), jnp.float32),
            vmem((cut, B), jnp.float32),
            vmem((8, B), jnp.int32),
            vmem((8, B), jnp.float32),
            vmem((rows, size), jnp.float32),
            pltpu.SMEM(live_from.shape, jnp.int32),
            pltpu.SMEM(noise_std.shape, jnp.float32),
            pltpu.SMEM(prior_info.shape, jnp.float32),
            dma((7,)),
            dma((nx - 1,)), dma((nx - 1,)),
            dma((NZ, nc - 1)), dma((NZ, nc - 1)),
            dma((NZ - 1,)), dma((NZ - 1,)),
            dma((ny // 2,)), dma((ny // 2,)),
            dma((NZ - 1,)), dma((NZ - 1,)),
            dma((NZ, nc - 1)), dma((NZ, nc - 1)),
        ],
        compiler_params=pltpu.CompilerParams(
            collective_id=0, has_side_effects=True, vmem_limit_bytes=56 * 2**20
        ),
        name="gather",
    )(tangent, well, live_from, noise_std, innovation, prior, prior_info)


def mm(a, b, dims):
    return lax.dot_general(
        stack(a, LEFT, dims[0][0]), stack(b, RIGHT, dims[1][0]), (dims, ((), ())), preferred_element_type=jnp.float32
    )


NN = ((1,), (0,))
NT = ((1,), (1,))


def stack(v, order, axis):
    parts = pieces(v)
    return jnp.concatenate([parts[k] for k in order], axis=axis)


LEFT, RIGHT = (0, 0, 1, 0, 2, 1), (0, 1, 0, 2, 0, 1)


def tn_pieces(a, b):
    return lax.dot_general(
        stack(a, LEFT, 0), stack(b, RIGHT, 0), (((0,), (0,)), ((), ())), preferred_element_type=jnp.float32
    )


def splat(row):
    return jnp.broadcast_to(row, (8, B))


def factor_block(s, width):
    tiles = width // 8
    sub = lax.broadcasted_iota(jnp.int32, (8, B), 0)
    lanes = lax.broadcasted_iota(jnp.int32, (B, B), 1)
    subs = lax.broadcasted_iota(jnp.int32, (B, B), 0)
    rest = jnp.concatenate([s, jnp.where(subs == lanes, 1.0, 0.0).astype(jnp.float32)], axis=1)
    done = []
    for lo in range(0, B, width):
        panel = [[rest[8 * t : 8 * t + 8, h * B : (h + 1) * B] for h in range(2)] for t in range(tiles)]
        pivots = [jnp.ones((8, B), jnp.float32) for _ in range(tiles)]

        def spread(g):
            at = lo + 8 * g
            return [
                [jnp.broadcast_to(panel[t][0][:, at + j : at + j + 1], (8, B)) if t >= g else None for t in range(tiles)]
                for j in range(8)
            ]

        columns = spread(0)
        for g in range(tiles):
            if g + 1 < tiles:
                columns = columns + spread(g + 1)
            for k in range(8 * g, 8 * g + 8, 2):
                r = k - 8 * g
                one, two = columns[k], columns[k + 1]
                a, b, c = splat(one[g][r : r + 1]), splat(one[g][r + 1 : r + 2]), splat(two[g][r + 1 : r + 2])
                det = a * c - b * b
                inverse, first = 1.0 / det, 1.0 / a
                pivots[g] = jnp.where(sub == r, a, jnp.where(sub == r + 1, det * first, pivots[g]))
                u = [(c * one[t] - b * two[t]) * inverse if t >= g else None for t in range(tiles)]
                v = [(a * two[t] - b * one[t]) * inverse if t >= g else None for t in range(tiles)]
                for j in range(k + 2, len(columns)):
                    tj, rj = divmod(j, 8)
                    p, q = splat(u[tj][rj : rj + 1]), splat(v[tj][rj : rj + 1])
                    for t in range(tj, tiles):
                        columns[j][t] = columns[j][t] - (one[t] * p + two[t] * q)
                u[g] = jnp.where(sub > r + 1, u[g], jnp.where(sub == r + 1, b * first, 0.0))
                v[g] = jnp.where(sub > r + 1, v[g], 0.0)
                for h in range(2):
                    p, q = splat(panel[g][h][r : r + 1]), splat(panel[g][h][r + 1 : r + 2])
                    for t in range(g, tiles):
                        panel[t][h] = panel[t][h] - (u[t] * p + v[t] * q)
        rows = jnp.concatenate(
            [
                jnp.concatenate([panel[t][h] * lax.rsqrt(pivots[t]) for h in range(2)], axis=1)
                for t in range(tiles)
            ],
            axis=0,
        )
        done.append(rows)
        if lo + width < B:
            rest = rest[width:] - tn_pieces(rows[:, :B], rows)[lo + width :]
    both = jnp.concatenate(done, axis=0)
    return jnp.where(subs <= lanes, both[:, :B], 0.0), both[:, B:]


def factorize(blocks, packed, ready, first, factor, answer):
    lanes = lax.broadcasted_iota(jnp.int32, (B, B), 1)
    subs = lax.broadcasted_iota(jnp.int32, (B, B), 0)
    lane = lax.broadcasted_iota(jnp.int32, (16, B), 1)
    s, vector = {}, []

    def take(k, i, j):
        tile = packed[k * B : (k + 1) * B, :]
        if i == j:
            vector.append(jnp.where(lane == B - 1, jnp.broadcast_to(tile[B - 2 : B - 1, 0:1], (16, B)), jnp.broadcast_to(tile[B - 1 : B, :], (16, B))))
            tile = jnp.where(subs <= lanes, tile, jnp.transpose(jnp.where(subs < lanes, tile, 0.0)))
        s[i, j] = tile

    assert first >= B
    take(0, 0, 0)
    factor[...] = jnp.zeros_like(factor)
    forward, inverse, right, back = [], [], {}, {}
    for i in range(blocks):
        lo, hi = i * B, (i + 1) * B
        r, t = factor_block(s[i, i], 32)
        factor[lo:hi, lo:hi] = r
        inverse.append(t)
        forward.append(mm(vector[i], t, NT))
        if i == 0:
            ready(blocks * B)
            for j in range(1, blocks):
                take(j, 0, j)
        if i + 1 < blocks:
            strip = mm(t, jnp.concatenate([s[i, j] for j in range(i + 1, blocks)], axis=1), NN)
            factor[lo:hi, hi:] = strip
            if i == 0:
                ready(packed.shape[0])
                for k, (p, q) in enumerate(pairs(blocks)):
                    if p:
                        take(k, p, q)
            for j in range(i + 1, blocks):
                at = (j - i - 1) * B
                right[i, j] = strip[:, at : at + B]
                back[i, j] = tn_pieces(right[i, j], t)
                update = tn_pieces(right[i, j], strip[:, at:])
                for k in range(j, blocks):
                    s[j, k] = s[j, k] - update[:, (k - j) * B : (k - j + 1) * B]
            update = mm(forward[i], strip, NN)
            for j in range(i + 1, blocks):
                vector[j] = vector[j] - update[:, (j - i - 1) * B : (j - i) * B]
    x = [None] * blocks
    for i in reversed(range(blocks)):
        x[i] = mm(forward[i], inverse[i], NN)
        for j in reversed(range(i + 1, blocks)):
            x[i] = x[i] - mm(x[j], back[i, j], NN)
        answer[8 * i : 8 * i + 8, :] = x[i][:8]


def body(nx, ny, tangent, well_of_obs, live_from, noise_std, innovation, prior_factor, prior_info):
    factor_rows, estimate_part = gathered(
        nx, ny, tangent, well_of_obs.reshape(-1, B), live_from, noise_std,
        innovation.reshape(-1, B), prior_factor, prior_info,
    )
    return (factor_rows[None, :, :], estimate_part)


def solution(mesh):
    in_specs = (P("gx", "gy"), P("gy"), P(), P(), P("gy"), P("gx", None), P())
    out_specs = (P("gy", "gx", None), P("gy", "gx"))
    nx, ny = mesh.shape["gx"], mesh.shape["gy"]
    return jax.shard_map(
        functools.partial(body, nx, ny), mesh=mesh, in_specs=in_specs, out_specs=out_specs, check_vma=False
    )
```
